512 devices in a mesh: dom: 128 (over x, z, core), sub: 4 (over y).
Axes of the slice: x: 4, y: 4, z: 16, core: 2. Of those that a mesh axis runs over, the one named last changes fastest.
Arguments:
- feats: bfloat16 [256, 49152], P('sub', 'dom'), may hold values from -6 to 6
- weight: bfloat16 [27, 256, 256], P(None, 'sub'), may hold values from -0.078125 to 0.078125
- grad_out: bfloat16 [256, 49152], P('sub', 'dom'), may hold values from -6 to 6
- neighbors: int32 [27, 49152], P(None, 'dom'), may hold values from -1 to 639, as said below
- send_rows: int32 [128, 256], P('dom'), may hold values from 0 to 383
- send_counts: int32 [128, 8], replicated, may hold values from 0 to 32, as said below
Outputs:
- out_feats: bfloat16 [256, 49152], P('sub', 'dom')
- grad_feats: float32 [256, 49152], P('sub', 'dom')
- grad_weight: float32 [27, 256, 256], P(None, 'sub')
The draws below stay inside these ranges and needn't reach their ends.
Inputs may be any that keep to these rules, and one draw needn't show every extreme that they name: neighbors[k, v] names the row of the table of v's partition that feeds v at offset k: values below 384 are the partition's own voxels, a value 384 + n * 32 + j names a received row with j below the count that arrives from direction n; -1 marks an absent neighbour; the middle offset names the voxel itself. send_counts[s, n] rows, the first ones of slots n * 32 onward of s's list, go from partition s to its neighbour in direction n; the count is 0 where that neighbour lies outside the grid, and positive otherwise.
All inputs are finite; a program needn't handle non-finite values.
Results may differ from the reference program's by a relative error of at most 0.001.
Values may be sent and summed in bfloat16 or wider, within the bound.
A program may use at most 64 MiB of HBM per device.

```python
import math
import jax
import jax.numpy as jnp
from jax import lax

C = 256
KVOL = 27
CAP = 32
V_DEV = 384
VOX = 49152
GRID_Y = 8
GRID_X = 16
HALO = 256
N_DOM = 128


DIRECTIONS = ((-1, -1), (-1, 0), (-1, 1), (0, -1), (0, 1), (1, -1), (1, 0), (1, 1))


def pair_counts(key):
    base = jax.random.fold_in(key, 4242)
    key_busy, key_low, key_high, key_full = jax.random.split(base, 4)
    busy = jax.random.randint(key_busy, (N_DOM,), 0, 4, dtype=jnp.int32) == 0
    lower = jax.random.randint(key_low, (N_DOM, 8), max(CAP // 4, 1), CAP // 2, dtype=jnp.int32)
    upper = jax.random.randint(key_high, (N_DOM, 8), CAP // 2, CAP + 1, dtype=jnp.int32)
    counts = jnp.where(busy[:, None], upper, lower)
    target = jax.random.randint(key_full, (N_DOM,), 0, 8, dtype=jnp.int32)
    column = jnp.arange(8, dtype=jnp.int32)[None, :]
    counts = jnp.where(column == target[:, None], CAP, counts)
    corner_source = (GRID_X - 2) * GRID_Y + GRID_Y - 2
    counts = counts.at[corner_source, 7].set(CAP)
    part_ids = jnp.arange(N_DOM, dtype=jnp.int32)
    place_x = part_ids // GRID_Y
    place_y = part_ids % GRID_Y
    valid_cols = []
    for step_x, step_y in DIRECTIONS:
        to_x = place_x + step_x
        to_y = place_y + step_y
        valid_cols.append((to_x >= 0) & (to_x < GRID_X) & (to_y >= 0) & (to_y < GRID_Y))
    valid = jnp.stack(valid_cols, axis=1)
    return jnp.where(valid, counts, 0).astype(jnp.int32)


def receive_counts(counts):
    part_ids = jnp.arange(N_DOM, dtype=jnp.int32)
    place_x = part_ids // GRID_Y
    place_y = part_ids % GRID_Y
    cols = []
    for direction, (step_x, step_y) in enumerate(DIRECTIONS):
        from_x = place_x - step_x
        from_y = place_y - step_y
        inside = (from_x >= 0) & (from_x < GRID_X) & (from_y >= 0) & (from_y < GRID_Y)
        source = jnp.where(inside, from_x * GRID_Y + from_y, 0).astype(jnp.int32)
        cols.append(jnp.where(inside, counts[source, direction], 0))
    return jnp.stack(cols, axis=1).astype(jnp.int32)


def draw_send_counts(key, part):
    return pair_counts(key)


def draw_neighbors(key, part):
    received = receive_counts(pair_counts(key))
    base = jax.random.fold_in(key, 977)
    key_kind, key_local, key_dir, key_slot = jax.random.split(base, 4)
    total_vox = N_DOM * V_DEV
    column = jnp.arange(total_vox, dtype=jnp.int32)
    owner = column // V_DEV
    kind = jax.random.randint(key_kind, (KVOL, total_vox), 0, 8, dtype=jnp.int32)
    local_pick = jax.random.randint(key_local, (KVOL, total_vox), 0, V_DEV, dtype=jnp.int32)
    dir_pick = jax.random.randint(key_dir, (KVOL, total_vox), 0, 8, dtype=jnp.int32)
    avail = received[owner[None, :], dir_pick]
    slot_pick = jax.random.randint(key_slot, (KVOL, total_vox), 0, jnp.maximum(avail, 1), dtype=jnp.int32)
    halo_pick = jnp.where(avail > 0, V_DEV + dir_pick * CAP + slot_pick, local_pick)
    chosen = jnp.where(kind < 4, -1, jnp.where(kind < 6, local_pick, halo_pick))
    offset_row = jnp.arange(KVOL, dtype=jnp.int32)[:, None]
    own = column % V_DEV
    chosen = jnp.where(offset_row == KVOL // 2, own[None, :], chosen)
    chosen = chosen.at[0, total_vox - 1].set(V_DEV + HALO - 1)
    return chosen.astype(jnp.int32)


def plant(entries, own_key, least, largest):
    longest = entries.shape.index(max(entries.shape))
    spots = []
    for shift in (0, 1):
        where = [jax.random.randint(jax.random.fold_in(own_key, axis), (), 0, length) for axis, length in enumerate(entries.shape)]
        where[longest] = (where[longest] + shift) % entries.shape[longest]
        spots.append(tuple(where))
    return entries.at[spots[0]].set(least).at[spots[1]].set(largest)


def steps_of(own_key, extent, shards, least, top_value):
    def one(position, shards_of):
        heights = jax.random.uniform(jax.random.fold_in(jax.random.fold_in(own_key, 6), position), (shards_of,), jnp.float32, least / len(shards), top_value / len(shards))
        return jnp.repeat(jnp.exp(heights), extent[position] // shards_of).reshape((-1,) + (1,) * (len(extent) - position - 1))

    gain = one(*shards[0])
    for cut in shards[1:]:
        gain = gain * one(*cut)
    return gain


def scatter_about(stream_key, extent, deviation, reach, cuts=(), kind=jnp.bfloat16):
    values = jax.random.normal(stream_key, extent, jnp.float32) * deviation
    if len(cuts) > 0:
        values = steps_of(stream_key, extent, cuts, -0.22, 0.18) * values
    return jnp.clip(values, min=-reach, max=reach).astype(kind)


def setup_inputs(seed: int = 0) -> dict:
    seeds = jax.random.split(jax.random.key(seed), 7)
    feats = scatter_about(seeds[0], (C, VOX), 1.0, 6.0, ((0, 4), (1, 128)))
    weight = scatter_about(seeds[1], (KVOL, C, C), (KVOL * C) ** -0.5, 0.078125, ((1, 4),))
    grad_out = scatter_about(seeds[2], (C, VOX), 1.0, 6.0, ((0, 4), (1, 128)))
    neighbors = draw_neighbors(jax.random.fold_in(seeds[6], 71), 0)
    send_rows = plant(jax.random.randint(seeds[4], (N_DOM, HALO), 0, V_DEV), jax.random.fold_in(seeds[4], 1), 0, V_DEV - 1).astype(jnp.int32)
    send_counts = draw_send_counts(jax.random.fold_in(seeds[6], 71), 0)
    return dict(feats=feats, weight=weight, grad_out=grad_out, neighbors=neighbors, send_rows=send_rows, send_counts=send_counts)


DIRECTIONS = ((-1, -1), (-1, 0), (-1, 1), (0, -1), (0, 1), (1, -1), (1, 0), (1, 1))

def reference(feats, weight, grad_out, neighbors, send_rows, send_counts):
    halo_cols = HALO
    part_ids = jnp.arange(N_DOM, dtype=jnp.int32)
    place_x = part_ids // GRID_Y
    place_y = part_ids % GRID_Y
    slot_ids = jnp.arange(CAP, dtype=jnp.int32)
    col_blocks = []
    live_blocks = []
    for direction, (step_x, step_y) in enumerate(DIRECTIONS):
        from_x = place_x - step_x
        from_y = place_y - step_y
        inside = (from_x >= 0) & (from_x < GRID_X) & (from_y >= 0) & (from_y < GRID_Y)
        source = jnp.where(inside, from_x * GRID_Y + from_y, 0).astype(jnp.int32)
        count_now = jnp.where(inside, send_counts[source, direction], 0)
        live_now = slot_ids[None, :] < count_now[:, None]
        rows_now = send_rows[source][:, direction * CAP:(direction + 1) * CAP]
        col_blocks.append(jnp.where(live_now, source[:, None] * V_DEV + rows_now, 0).astype(jnp.int32))
        live_blocks.append(live_now)
    global_col = jnp.concatenate(col_blocks, axis=1).astype(jnp.int32)
    live = jnp.concatenate(live_blocks, axis=1)
    part_feats = feats.reshape(C, N_DOM, V_DEV).transpose(1, 0, 2)
    part_grad = grad_out.reshape(C, N_DOM, V_DEV).transpose(1, 0, 2)
    part_nbr = neighbors.reshape(KVOL, N_DOM, V_DEV).transpose(1, 0, 2)
    weight_wide = weight.astype(jnp.float32)

    def visit(wgrad_sum, inputs):
        local_feats, local_grad, local_nbr, cols, col_live = inputs
        halo_feats = jnp.where(col_live[None, :], feats[:, cols], jnp.zeros((), feats.dtype))
        table = jnp.concatenate([local_feats, halo_feats], axis=1)
        grad_wide = local_grad.astype(jnp.float32)
        out_sum = jnp.zeros((C, V_DEV), jnp.float32)
        table_grad = jnp.zeros((C, V_DEV + halo_cols), jnp.float32)
        for offset in range(KVOL):
            nbr_now = local_nbr[offset]
            nbr_live = nbr_now >= 0
            nbr_safe = jnp.maximum(nbr_now, 0).astype(jnp.int32)
            picked = jnp.where(nbr_live[None, :], table[:, nbr_safe], jnp.zeros((), table.dtype)).astype(jnp.float32)
            out_sum = out_sum + jnp.dot(weight_wide[offset], picked)
            wgrad_sum = wgrad_sum.at[offset].add(jnp.dot(grad_wide, picked.T))
            spread = jnp.dot(weight_wide[offset].T, grad_wide)
            table_grad = table_grad.at[:, nbr_safe].add(jnp.where(nbr_live[None, :], spread, jnp.zeros((), jnp.float32)))
        return (wgrad_sum, (out_sum.astype(jnp.bfloat16), table_grad))
    wgrad_total, (out_parts, grad_parts) = lax.scan(visit, jnp.zeros((KVOL, C, C), jnp.float32), (part_feats, part_grad, part_nbr, global_col, live))
    out_feats = out_parts.transpose(1, 0, 2).reshape(C, N_DOM * V_DEV)
    local_grad = grad_parts[:, :, :V_DEV].transpose(1, 0, 2).reshape(C, N_DOM * V_DEV)
    halo_vals = grad_parts[:, :, V_DEV:].transpose(1, 0, 2).reshape(C, N_DOM * halo_cols)
    flat_live = live.reshape(-1)
    grad_feats = local_grad.at[:, global_col.reshape(-1)].add(jnp.where(flat_live[None, :], halo_vals, jnp.zeros((), jnp.float32)))
    grad_weight = wgrad_total * (1.0 / math.sqrt(N_DOM * V_DEV))
    return (out_feats, grad_feats, grad_weight)
```

```python
import math

import jax
import jax.numpy as jnp
from jax import lax
from jax.experimental import pallas as pl
from jax.experimental.pallas import tpu as pltpu
from jax.sharding import PartitionSpec as P

C = 256
KVOL = 27
CAP = 32
SUB = 4
NX = 4
NZ = 16
DOM = 2 * NX * NZ
SHARE = C // SUB
VOX = 384
HALO = 8 * CAP
COLS = VOX + HALO
GRID_Y = 8
DIRECTIONS = ((-1, -1), (-1, 0), (-1, 1), (0, -1), (0, 1), (1, -1), (1, 0), (1, 1))
HOPS = tuple(dx * GRID_Y + dy for dx, dy in DIRECTIONS)
CHUNKS = ((0, 15), (15, 27))
UNROLL = 3
STEPS = 128.0
TOP = 32000.0
MESH = pl.DeviceIdType.MESH
F32 = jnp.float32
BF16 = jnp.bfloat16
I16 = jnp.int16


def dot(a, b, dims):
    return lax.dot_general(a, b, (dims, ((), ())), preferred_element_type=F32)


NN = ((1,), (0,))
NT = ((1,), (1,))
TN = ((0,), (0,))


def encode(tiles, n):
    row = lax.broadcasted_iota(jnp.int32, tiles.shape, tiles.ndim - 2)
    tiles = jnp.where(row < n, tiles, 0.0)
    top = jnp.max(jnp.abs(tiles), axis=-2, keepdims=True)
    level = jnp.ceil(jnp.log2(jnp.maximum(top, 1e-33)) * STEPS)
    codes = jnp.round(tiles * (jnp.exp2(level * (-1.0 / STEPS)) * TOP))
    return jnp.where(row == n, level, codes).astype(jnp.int32).astype(I16)


def decode(codes, n):
    values = codes.astype(jnp.int32).astype(F32)
    level = values[..., n : n + 1, :]
    return values * (jnp.exp2(level * (1.0 / STEPS)) * (1.0 / TOP))


def kernel(
    feats, weight, grad_out, neighbors, send_rows, send_counts,
    out_feats, grad_feats, codes,
    nbr_t, onehot, picked, spread_hi, spread_lo, share_all, halo_out, halo_in, halo_all,
    table, wg, pair_in, x_out, x_in, x_sum, z_out, z_in, tg, tg_in, back_out, back_in,
    send, recv,
):
    me = lax.axis_index("dom")
    sub = lax.axis_index("sub")
    core = lax.rem(me, 2)
    z = lax.rem(me // 2, NZ)
    x = me // (2 * NZ)

    def wrap(i):
        return lax.rem(i + DOM, DOM)

    def at(xx, zz, cc):
        return (xx * NZ + zz) * 2 + cc

    twin = at(x, z, 1 - core)

    def x_peer(d):
        return lax.rem(x + d, NX)

    def z_peer(d):
        return lax.rem(z + d, NZ)

    def y_peer(d):
        return lax.rem(sub + d, SUB)

    slots = {}

    def copy(name, index, src, dst, device):
        base = slots[name]
        return pltpu.make_async_remote_copy(
            src_ref=src, dst_ref=dst, send_sem=send.at[base + index], recv_sem=recv.at[base + index],
            device_id=device, device_id_type=MESH,
        )

    for base, name in enumerate(("share", "fwd", "tg")):
        slots[name] = 3 * base
    slots["halo"], slots["back"] = 9, 17
    slots["pair"], slots["gpair"] = 25, 27
    slots["x"], slots["gx"] = 29, 35
    slots["z"], slots["gz"] = 41, 73

    barrier = pltpu.get_barrier_semaphore()
    peers = [(me, y_peer(d)) for d in range(1, SUB)]
    peers += [(wrap(me + hop), sub) for hop in HOPS]
    peers += [(twin, sub)]
    peers += [(at(x_peer(d), z, core), sub) for d in range(1, NX)]
    with jax.named_scope("barrier_signals"):
        for peer in peers:
            pl.semaphore_signal(barrier, inc=1, device_id=peer, device_id_type=MESH)

        @pl.loop(1, NZ)
        def _(d):
            pl.semaphore_signal(barrier, inc=1, device_id=(at(x, z_peer(d), core), sub), device_id_type=MESH)

    with jax.named_scope("boundary_tiles"):
        lane = lax.broadcasted_iota(jnp.int32, (1, HALO), 1)
        mine = send_counts[...]
        mine = jnp.where(lax.broadcasted_iota(jnp.int32, (8, DOM), 1) == me, mine, 0).astype(F32)
        mine = jnp.sum(mine, axis=1, keepdims=True).astype(jnp.int32)
        count = jnp.zeros((1, HALO), jnp.int32)
        for n in range(8):
            count = jnp.where(lane // CAP == n, mine[n : n + 1, :], count)
        rows = jnp.where(lane % CAP < count, send_rows[...], -1)
        pick = (lax.broadcasted_iota(jnp.int32, (VOX, HALO), 0) == rows).astype(F32).astype(BF16)
        outgoing = dot(feats[...], pick, NN).T.reshape(8, 2, 16, SHARE)
        halo_out[...] = jnp.concatenate([outgoing[:, 0], outgoing[:, 1]], axis=-1).astype(BF16)

    with jax.named_scope("barrier_wait"):
        pl.semaphore_wait(barrier, len(peers) + NZ - 1)

    def share_copy(d):
        return copy("share", d - 1, feats, share_all.at[sub], (me, y_peer(d)))

    def halo_copy(n):
        return copy("halo", n, halo_out.at[n], halo_in.at[n], (wrap(me + HOPS[n]), sub))

    def fwd_copy(d):
        return copy("fwd", d - 1, halo_in, halo_all.at[sub], (me, y_peer(d)))

    with jax.named_scope("first_sends"):
        for n in range(8):
            halo_copy(n).start()
        for d in range(1, SUB):
            share_copy(d).start()
        share_all[sub] = feats[...]

    with jax.named_scope("transpose_maps"):
        nbr_t[...] = jnp.concatenate(
            [neighbors[...], jnp.zeros((128 - KVOL, VOX), jnp.int32)], axis=0
        ).T
        col = lax.broadcasted_iota(jnp.int32, (1, COLS), 1)
        r = col - VOX
        slot = jnp.where(col < VOX, col, VOX + ((r % 128) // 16) * CAP + (r // 128) * 16 + r % 16)
        spread_hi[KVOL] = jnp.zeros((SHARE, COLS), BF16)
        spread_lo[KVOL] = jnp.zeros((SHARE, COLS), BF16)

    with jax.named_scope("onehot_and_spread"):
        @pl.loop(0, KVOL // UNROLL)
        def _(g):
            now = nbr_t[...]
            nbr_t[...] = pltpu.roll(now, 128 - UNROLL, 1)
            for j in range(UNROLL):
                k = g * UNROLL + j
                hot = (now[:, j : j + 1] == slot).astype(F32).astype(BF16)
                onehot[k] = hot
                total = dot(grad_out[...], hot, NN)
                high = total.astype(BF16)
                spread_hi[k] = high
                spread_lo[k] = (total - high.astype(F32)).astype(BF16)

    with jax.named_scope("halo_arrival"):
        for n in range(8):
            halo_copy(n).wait_recv()
        for d in range(1, SUB):
            fwd_copy(d).start()
        halo_all[sub] = halo_in[...]

    with jax.named_scope("table_grad"):
        total = None
        for k in range(0, KVOL, 4):
            n = min(4, KVOL - k)
            w = weight[k : k + n].reshape(n * SHARE, C)
            for part in (spread_hi, spread_lo):
                term = dot(w, part[k : k + n].reshape(n * SHARE, COLS), TN)
                total = term if total is None else total + term
        tg[...] = total.reshape(SUB, SHARE, COLS)

    def tg_copy(d):
        return copy("tg", d - 1, tg.at[y_peer(d)], tg_in.at[d - 1], (me, y_peer(d)))

    with jax.named_scope("tg_sends"):
        for d in range(1, SUB):
            tg_copy(d).start()

    with jax.named_scope("table"):
        for d in range(1, SUB):
            share_copy(d).wait_recv()
        table[0:VOX] = share_all[...].reshape(C, VOX).T
        for d in range(1, SUB):
            fwd_copy(d).wait_recv()
        tiles = halo_all[...].reshape(SUB, 128, 128)
        for half in range(2):
            lanes = slice(half * SHARE, (half + 1) * SHARE)
            table[VOX + half * 128 : VOX + (half + 1) * 128] = jnp.concatenate(
                [tiles[s][:, lanes] for s in range(SUB)], axis=1
            )

    def pair_copy(c):
        return copy("pair", c, wg.at[c, 1 - core], pair_in.at[c], (twin, sub))

    def x_copy(c, d):
        return copy("x", 3 * c + d - 1, x_out.at[c, x_peer(d)], x_in.at[c, d - 1], (at(x_peer(d), z, core), sub))

    def own_tile(zz):
        return pl.ds(pl.multiple_of(zz * 16, 16), 16)

    def z_copy(c, d):
        return copy("z", 16 * c + d - 1, z_out.at[c, own_tile(z_peer(d))], z_in.at[c, d - 1], (at(x, z_peer(d), core), sub))

    def gz_copy(c, d):
        ref = codes.at[c, core, x, own_tile(z)]
        return copy("gz", 16 * c + d - 1, ref, ref, (at(x, z_peer(d), core), sub))

    def gz_arrival(c, d):
        ref = codes.at[c, core, x, own_tile(z_peer(NZ - d))]
        return copy("gz", 16 * c + d - 1, ref, ref, (at(x, z_peer(d), core), sub))

    def gx_copy(c, d):
        ref = codes.at[c, core, x]
        return copy("gx", 3 * c + d - 1, ref, ref, (at(x_peer(d), z, core), sub))

    def gx_arrival(c, d):
        ref = codes.at[c, core, x_peer(NX - d)]
        return copy("gx", 3 * c + d - 1, ref, ref, (at(x_peer(d), z, core), sub))

    def gpair_copy(c):
        ref = codes.at[c, core]
        return copy("gpair", c, ref, ref, (twin, sub))

    def gpair_arrival(c):
        ref = codes.at[c, 1 - core]
        return copy("gpair", c, ref, ref, (twin, sub))

    def gather(c, first, last):
        lo = CHUNKS[c][0]

        @pl.loop(first // UNROLL, last // UNROLL)
        def _(g):
            k0 = g * UNROLL
            hot = onehot[pl.ds(k0, UNROLL)].reshape(UNROLL * VOX, COLS)
            got = dot(hot, table[...], NN).astype(BF16).reshape(UNROLL, VOX, C)
            picked[pl.ds(k0, UNROLL)] = got
            for j in range(UNROLL):
                fresh = dot(grad_out[...], got[j], NN)
                for cc in range(2):
                    for xx in range(NX):
                        r0, l0 = cc * 32 + (xx // 2) * 16, (xx % 2) * 128
                        wg[c, cc, xx, pl.ds(k0 + j - lo, 16, stride=16), :] = fresh[r0 : r0 + 16, l0 : l0 + 128]

    def pair_to_x(c):
        lo, hi = CHUNKS[c]
        pair_copy(c).wait_recv()
        for xx in range(NX):
            both = wg[c, core, xx] + pair_in[c, xx]
            x_out[c, xx] = encode(both.reshape(16, 16, 128), hi - lo).reshape(256, 128)
        for d in range(1, NX):
            x_copy(c, d).start()

    def x_to_z(c):
        lo, hi = CHUNKS[c]
        for d in range(1, NX):
            x_copy(c, d).wait_recv()
        total = (wg[c, core, x] + pair_in[c, x]).reshape(16, 16, 128)
        for d in range(1, NX):
            total = total + decode(x_in[c, d - 1].reshape(16, 16, 128), hi - lo)
        x_sum[c] = total.reshape(256, 128)
        z_out[c] = encode(total, hi - lo).reshape(256, 128)

        @pl.loop(1, NZ)
        def _(d):
            z_copy(c, d).start()

    with jax.named_scope("wg_rows"):
        for c, (lo, hi) in enumerate(CHUNKS):
            for row in range(hi - lo, 16):
                for cc in range(2):
                    for xx in range(NX):
                        wg[c, cc, xx, pl.ds(row, 16, stride=16), :] = jnp.zeros((16, 128), F32)

    with jax.named_scope("gather_a"):
        gather(0, 0, 15)
    with jax.named_scope("pair_a"):
        pair_copy(0).start()
    with jax.named_scope("gather_b"):
        gather(1, 15, 21)
    with jax.named_scope("pair_to_x_a"):
        pair_to_x(0)
    with jax.named_scope("gather_c"):
        gather(1, 21, 27)
    with jax.named_scope("pair_b"):
        pair_copy(1).start()

    with jax.named_scope("tg_sum"):
        for d in range(1, SUB):
            tg_copy(d).wait_recv()
        mine_tg = tg[sub] + tg_in[0] + tg_in[1] + tg_in[2]
        tail = mine_tg[:, VOX:].T
        back_out[...] = jnp.concatenate([tail[:128], tail[128:]], axis=1).reshape(8, 16, 128)

    def back_copy(n):
        return copy("back", n, back_out.at[n], back_in.at[n], (wrap(me - HOPS[n]), sub))

    with jax.named_scope("back_sends"):
        for n in range(8):
            back_copy(n).start()

    with jax.named_scope("x_to_z_a"):
        x_to_z(0)
    with jax.named_scope("pair_to_x_b"):
        pair_to_x(1)

    with jax.named_scope("out_feats"):
        def out_step(g, acc):
            for j in range(UNROLL):
                acc = acc + dot(weight[g * UNROLL + j], picked[g * UNROLL + j], NT)
            return acc

        out_feats[...] = lax.fori_loop(0, KVOL // UNROLL, out_step, jnp.zeros((SHARE, VOX), F32)).astype(BF16)

    with jax.named_scope("x_to_z_b"):
        x_to_z(1)

    with jax.named_scope("grad_feats"):
        for n in range(8):
            back_copy(n).wait_recv()
        back = back_in[...]
        back = jnp.concatenate([back[:, :, :SHARE][:, None], back[:, :, SHARE:][:, None]], axis=1)
        back = back.reshape(HALO, SHARE).T
        back_hi = back.astype(BF16)
        back_lo = (back - back_hi.astype(F32)).astype(BF16)
        grad_feats[...] = mine_tg[:, :VOX] + dot(back_hi, pick, NT) + dot(back_lo, pick, NT)

    def z_reduce(c):
        lo, hi = CHUNKS[c]

        @pl.loop(1, NZ)
        def _(d):
            z_copy(c, d).wait_recv()

        total = x_sum[c, own_tile(z)] + jnp.sum(decode(z_in[c], hi - lo), axis=0)
        scaled = total * (1.0 / math.sqrt(VOX * DOM))
        codes[c, core, x, own_tile(z)] = encode(scaled, hi - lo)

        @pl.loop(1, NZ)
        def _(d):
            gz_copy(c, d).start()

    def z_to_x(c):
        @pl.loop(1, NZ)
        def _(d):
            gz_arrival(c, d).wait_recv()

        for d in range(1, NX):
            gx_copy(c, d).start()

    def x_to_pair(c):
        for d in range(1, NX):
            gx_arrival(c, d).wait_recv()
        gpair_copy(c).start()

    with jax.named_scope("z_reduce_a"):
        z_reduce(0)
    with jax.named_scope("z_reduce_b"):
        z_reduce(1)
    with jax.named_scope("z_back"):
        z_to_x(0)
        z_to_x(1)
    with jax.named_scope("x_back"):
        x_to_pair(0)
        x_to_pair(1)
    with jax.named_scope("pair_back"):
        gpair_arrival(0).wait_recv()
        gpair_arrival(1).wait_recv()

    with jax.named_scope("drain"):
        for d in range(1, SUB):
            share_copy(d).wait_send()
            fwd_copy(d).wait_send()
            tg_copy(d).wait_send()
        for n in range(8):
            halo_copy(n).wait_send()
            back_copy(n).wait_send()
        for c in range(2):
            pair_copy(c).wait_send()
            gpair_copy(c).wait_send()
            for d in range(1, NX):
                x_copy(c, d).wait_send()
                gx_copy(c, d).wait_send()

            @pl.loop(1, NZ)
            def _(d):
                z_copy(c, d).wait_send()
                gz_copy(c, d).wait_send()


def finish(codes, out_in, feats_in, out_feats, grad_feats, grad_weight):
    out_feats[...] = out_in[...]
    grad_feats[...] = feats_in[...]
    for c, (lo, hi) in enumerate(CHUNKS):
        for cc in range(2):
            for xx in range(NX):
                values = decode(codes[c, cc, xx].reshape(16, 16, 128), hi - lo)
                r0, l0 = cc * 32 + (xx // 2) * 16, (xx % 2) * 128
                values = jnp.swapaxes(values, 0, 1)
                grad_weight[lo:hi, r0 : r0 + 16, l0 : l0 + 128] = values[: hi - lo]


def body(feats, weight, grad_out, neighbors, send_rows, send_counts):
    vmem = pl.BlockSpec(memory_space=pltpu.VMEM)
    out_feats, grad_feats, codes = pl.pallas_call(
        kernel,
        out_shape=(
            jax.ShapeDtypeStruct((SHARE, VOX), BF16),
            jax.ShapeDtypeStruct((SHARE, VOX), F32),
            jax.ShapeDtypeStruct((2, 2, NX, 256, 128), I16),
        ),
        in_specs=[vmem] * 6,
        out_specs=[vmem] * 3,
        scratch_shapes=[
            pltpu.VMEM((VOX, 128), jnp.int32),
            pltpu.VMEM((KVOL, VOX, COLS), BF16),
            pltpu.VMEM((KVOL, VOX, C), BF16),
            pltpu.VMEM((KVOL + 1, SHARE, COLS), BF16),
            pltpu.VMEM((KVOL + 1, SHARE, COLS), BF16),
            pltpu.VMEM((SUB, SHARE, VOX), BF16),
            pltpu.VMEM((8, 16, 128), BF16),
            pltpu.VMEM((8, 16, 128), BF16),
            pltpu.VMEM((SUB, 8, 16, 128), BF16),
            pltpu.VMEM((COLS, C), BF16),
            pltpu.VMEM((2, 2, NX, 256, 128), F32),
            pltpu.VMEM((2, NX, 256, 128), F32),
            pltpu.VMEM((2, NX, 256, 128), I16),
            pltpu.VMEM((2, NX - 1, 256, 128), I16),
            pltpu.VMEM((2, 256, 128), F32),
            pltpu.VMEM((2, 256, 128), I16),
            pltpu.VMEM((2, NZ - 1, 16, 128), I16),
            pltpu.VMEM((SUB, SHARE, COLS), F32),
            pltpu.VMEM((SUB - 1, SHARE, COLS), F32),
            pltpu.VMEM((8, 16, 128), F32),
            pltpu.VMEM((8, 16, 128), F32),
            pltpu.SemaphoreType.DMA((105,)),
            pltpu.SemaphoreType.DMA((105,)),
        ],
        compiler_params=pltpu.CompilerParams(
            collective_id=0, has_side_effects=True, vmem_limit_bytes=56 * 1024 * 1024
        ),
    )(feats, weight, grad_out, neighbors, send_rows, send_counts.T)
    return pl.pallas_call(
        finish,
        out_shape=(
            jax.ShapeDtypeStruct((SHARE, VOX), BF16),
            jax.ShapeDtypeStruct((SHARE, VOX), F32),
            jax.ShapeDtypeStruct((KVOL, SHARE, C), F32),
        ),
        in_specs=[vmem] * 3,
        out_specs=[vmem] * 3,
        compiler_params=pltpu.CompilerParams(vmem_limit_bytes=32 * 1024 * 1024),
    )(codes, out_feats, grad_feats)


def solution(mesh):
    in_specs = (
        P("sub", "dom"),
        P(None, "sub", None),
        P("sub", "dom"),
        P(None, "dom"),
        P("dom", None),
        P(),
    )
    out_specs = (P("sub", "dom"), P("sub", "dom"), P(None, "sub", None))
    return jax.shard_map(body, mesh=mesh, in_specs=in_specs, out_specs=out_specs, check_vma=False)
```

```python
import math

import jax
import jax.numpy as jnp
from jax import lax
from jax.experimental import pallas as pl
from jax.experimental.pallas import tpu as pltpu
from jax.sharding import PartitionSpec as P

C = 256
KVOL = 27
CAP = 32
SUB = 4
NX = 4
NZ = 16
DOM = 2 * NX * NZ
SHARE = C // SUB
VOX = 384
HALO = 8 * CAP
COLS = VOX + HALO
GRID_Y = 8
DIRECTIONS = ((-1, -1), (-1, 0), (-1, 1), (0, -1), (0, 1), (1, -1), (1, 0), (1, 1))
HOPS = tuple(dx * GRID_Y + dy for dx, dy in DIRECTIONS)
CHUNKS = ((0, 15), (15, 27))
UNROLL = 3
STEPS = 128.0
TOP = 32000.0
MESH = pl.DeviceIdType.MESH
F32 = jnp.float32
BF16 = jnp.bfloat16
I16 = jnp.int16


def dot(a, b, dims):
    return lax.dot_general(a, b, (dims, ((), ())), preferred_element_type=F32)


NN = ((1,), (0,))
NT = ((1,), (1,))
TN = ((0,), (0,))


def encode(tiles, n):
    row = lax.broadcasted_iota(jnp.int32, tiles.shape, tiles.ndim - 2)
    tiles = jnp.where(row < n, tiles, 0.0)
    top = jnp.max(jnp.abs(tiles), axis=-2, keepdims=True)
    level = jnp.ceil(jnp.log2(jnp.maximum(top, 1e-33)) * STEPS)
    codes = jnp.round(tiles * (jnp.exp2(level * (-1.0 / STEPS)) * TOP))
    return jnp.where(row == n, level, codes).astype(jnp.int32).astype(I16)


def decode(codes, n):
    values = codes.astype(jnp.int32).astype(F32)
    level = values[..., n : n + 1, :]
    return values * (jnp.exp2(level * (1.0 / STEPS)) * (1.0 / TOP))


def kernel(
    feats, weight, grad_out, neighbors, send_rows, send_counts,
    out_feats, grad_feats, codes,
    nbr_t, onehot, picked, spread_hi, spread_lo, share_all, halo_out, halo_in, halo_all,
    table, wg, pair_in, x_out, x_in, x_sum, z_out, z_in, tg, tg_in, back_out, back_in,
    send, recv,
):
    me = lax.axis_index("dom")
    sub = lax.axis_index("sub")
    core = lax.rem(me, 2)
    z = lax.rem(me // 2, NZ)
    x = me // (2 * NZ)

    def wrap(i):
        return lax.rem(i + DOM, DOM)

    def at(xx, zz, cc):
        return (xx * NZ + zz) * 2 + cc

    twin = at(x, z, 1 - core)

    def x_peer(d):
        return lax.rem(x + d, NX)

    def z_peer(d):
        return lax.rem(z + d, NZ)

    def y_peer(d):
        return lax.rem(sub + d, SUB)

    slots = {}

    def copy(name, index, src, dst, device):
        base = slots[name]
        return pltpu.make_async_remote_copy(
            src_ref=src, dst_ref=dst, send_sem=send.at[base + index], recv_sem=recv.at[base + index],
            device_id=device, device_id_type=MESH,
        )

    for base, name in enumerate(("share", "fwd", "tg")):
        slots[name] = 3 * base
    slots["halo"], slots["back"] = 9, 17
    slots["pair"], slots["gpair"] = 25, 27
    slots["x"], slots["gx"] = 29, 35
    slots["z"], slots["gz"] = 41, 73

    barrier = pltpu.get_barrier_semaphore()
    peers = [(me, y_peer(d)) for d in range(1, SUB)]
    peers += [(wrap(me + hop), sub) for hop in HOPS]
    peers += [(twin, sub)]
    peers += [(at(x_peer(d), z, core), sub) for d in range(1, NX)]
    with jax.named_scope("barrier_signals"):
        for peer in peers:
            pl.semaphore_signal(barrier, inc=1, device_id=peer, device_id_type=MESH)

        @pl.loop(1, NZ)
        def _(d):
            pl.semaphore_signal(barrier, inc=1, device_id=(at(x, z_peer(d), core), sub), device_id_type=MESH)

    with jax.named_scope("boundary_tiles"):
        lane = lax.broadcasted_iota(jnp.int32, (1, HALO), 1)
        mine = send_counts[...]
        mine = jnp.where(lax.broadcasted_iota(jnp.int32, (8, DOM), 1) == me, mine, 0).astype(F32)
        mine = jnp.sum(mine, axis=1, keepdims=True).astype(jnp.int32)
        count = jnp.zeros((1, HALO), jnp.int32)
        for n in range(8):
            count = jnp.where(lane // CAP == n, mine[n : n + 1, :], count)
        rows = jnp.where(lane % CAP < count, send_rows[...], -1)
        pick = (lax.broadcasted_iota(jnp.int32, (VOX, HALO), 0) == rows).astype(F32).astype(BF16)
        outgoing = dot(feats[...], pick, NN).T.reshape(8, 2, 16, SHARE)
        halo_out[...] = jnp.concatenate([outgoing[:, 0], outgoing[:, 1]], axis=-1).astype(BF16)

    with jax.named_scope("barrier_wait"):
        pl.semaphore_wait(barrier, len(peers) + NZ - 1)

    def share_copy(d):
        return copy("share", d - 1, feats, share_all.at[sub], (me, y_peer(d)))

    def halo_copy(n):
        return copy("halo", n, halo_out.at[n], halo_in.at[n], (wrap(me + HOPS[n]), sub))

    def fwd_copy(d):
        return copy("fwd", d - 1, halo_in, halo_all.at[sub], (me, y_peer(d)))

    with jax.named_scope("first_sends"):
        for n in range(8):
            halo_copy(n).start()
        for d in range(1, SUB):
            share_copy(d).start()
        share_all[sub] = feats[...]

    with jax.named_scope("transpose_maps"):
        nbr_t[...] = jnp.concatenate(
            [neighbors[...], jnp.zeros((128 - KVOL, VOX), jnp.int32)], axis=0
        ).T
        col = lax.broadcasted_iota(jnp.int32, (1, COLS), 1)
        r = col - VOX
        slot = jnp.where(col < VOX, col, VOX + ((r % 128) // 16) * CAP + (r // 128) * 16 + r % 16)

    with jax.named_scope("onehot"):
        @pl.loop(0, KVOL // UNROLL)
        def _(g):
            now = nbr_t[...]
            nbr_t[...] = pltpu.roll(now, 128 - UNROLL, 1)
            for j in range(UNROLL):
                onehot[g * UNROLL + j] = (now[:, j : j + 1] == slot).astype(F32).astype(BF16)

    def gather_own(first, last):
        @pl.loop(first // UNROLL, last // UNROLL)
        def _(g):
            hot = onehot[pl.ds(g * UNROLL, UNROLL), :, 0:VOX].reshape(UNROLL * VOX, VOX)
            got = dot(hot, table[0:VOX], NN).astype(BF16)
            picked[pl.ds(g * UNROLL, UNROLL)] = got.reshape(UNROLL, VOX, C)

    with jax.named_scope("table_own"):
        for d in range(1, SUB):
            share_copy(d).wait_recv()
        table[0:VOX] = share_all[...].reshape(C, VOX).T
    with jax.named_scope("gather_own_a"):
        gather_own(0, 15)

    with jax.named_scope("halo_arrival"):
        for n in range(8):
            halo_copy(n).wait_recv()
        for d in range(1, SUB):
            fwd_copy(d).start()
        halo_all[sub] = halo_in[...]

    with jax.named_scope("gather_own_b"):
        gather_own(15, 27)

    with jax.named_scope("table_halo"):
        for d in range(1, SUB):
            fwd_copy(d).wait_recv()
        tiles = halo_all[...].reshape(SUB, 128, 128)
        for half in range(2):
            lanes = slice(half * SHARE, (half + 1) * SHARE)
            table[VOX + half * 128 : VOX + (half + 1) * 128] = jnp.concatenate(
                [tiles[s][:, lanes] for s in range(SUB)], axis=1
            )

    def pair_copy(c):
        return copy("pair", c, wg.at[c, 1 - core], pair_in.at[c], (twin, sub))

    def x_copy(c, d):
        return copy("x", 3 * c + d - 1, x_out.at[c, x_peer(d)], x_in.at[c, d - 1], (at(x_peer(d), z, core), sub))

    def own_tile(zz):
        return pl.ds(pl.multiple_of(zz * 16, 16), 16)

    def z_copy(c, d):
        return copy("z", 16 * c + d - 1, z_out.at[c, own_tile(z_peer(d))], z_in.at[c, d - 1], (at(x, z_peer(d), core), sub))

    def gz_copy(c, d):
        ref = codes.at[c, core, x, own_tile(z)]
        return copy("gz", 16 * c + d - 1, ref, ref, (at(x, z_peer(d), core), sub))

    def gz_arrival(c, d):
        ref = codes.at[c, core, x, own_tile(z_peer(NZ - d))]
        return copy("gz", 16 * c + d - 1, ref, ref, (at(x, z_peer(d), core), sub))

    def gx_copy(c, d):
        ref = codes.at[c, core, x]
        return copy("gx", 3 * c + d - 1, ref, ref, (at(x_peer(d), z, core), sub))

    def gx_arrival(c, d):
        ref = codes.at[c, core, x_peer(NX - d)]
        return copy("gx", 3 * c + d - 1, ref, ref, (at(x_peer(d), z, core), sub))

    def gpair_copy(c):
        ref = codes.at[c, core]
        return copy("gpair", c, ref, ref, (twin, sub))

    def gpair_arrival(c):
        ref = codes.at[c, 1 - core]
        return copy("gpair", c, ref, ref, (twin, sub))

    def gather(c, first, last):
        lo = CHUNKS[c][0]

        @pl.loop(first // UNROLL, last // UNROLL)
        def _(g):
            k0 = g * UNROLL
            hot = onehot[pl.ds(k0, UNROLL), :, VOX:COLS].reshape(UNROLL * VOX, HALO)
            got = dot(hot, table[VOX:COLS], NN).astype(BF16).reshape(UNROLL, VOX, C)
            got = got + picked[pl.ds(k0, UNROLL)]
            picked[pl.ds(k0, UNROLL)] = got
            for j in range(UNROLL):
                fresh = dot(grad_out[...], got[j], NN)
                for cc in range(2):
                    for xx in range(NX):
                        r0, l0 = cc * 32 + (xx // 2) * 16, (xx % 2) * 128
                        wg[c, cc, xx, pl.ds(k0 + j - lo, 16, stride=16), :] = fresh[r0 : r0 + 16, l0 : l0 + 128]

    def pair_to_x(c):
        lo, hi = CHUNKS[c]
        pair_copy(c).wait_recv()
        for xx in range(NX):
            both = wg[c, core, xx] + pair_in[c, xx]
            x_out[c, xx] = encode(both.reshape(16, 16, 128), hi - lo).reshape(256, 128)
        for d in range(1, NX):
            x_copy(c, d).start()

    def x_to_z(c):
        lo, hi = CHUNKS[c]
        for d in range(1, NX):
            x_copy(c, d).wait_recv()
        total = (wg[c, core, x] + pair_in[c, x]).reshape(16, 16, 128)
        for d in range(1, NX):
            total = total + decode(x_in[c, d - 1].reshape(16, 16, 128), hi - lo)
        x_sum[c] = total.reshape(256, 128)
        z_out[c] = encode(total, hi - lo).reshape(256, 128)

        @pl.loop(1, NZ)
        def _(d):
            z_copy(c, d).start()

    with jax.named_scope("wg_rows"):
        for c, (lo, hi) in enumerate(CHUNKS):
            for row in range(hi - lo, 16):
                for cc in range(2):
                    for xx in range(NX):
                        wg[c, cc, xx, pl.ds(row, 16, stride=16), :] = jnp.zeros((16, 128), F32)

    with jax.named_scope("gather_a"):
        gather(0, 0, 15)
    with jax.named_scope("pair_a"):
        pair_copy(0).start()
    with jax.named_scope("gather_b"):
        gather(1, 15, 21)
    with jax.named_scope("pair_to_x_a"):
        pair_to_x(0)
    with jax.named_scope("gather_c"):
        gather(1, 21, 27)
    with jax.named_scope("pair_b"):
        pair_copy(1).start()

    with jax.named_scope("x_to_z_a"):
        x_to_z(0)
    with jax.named_scope("pair_to_x_b"):
        pair_to_x(1)

    with jax.named_scope("spread"):
        @pl.loop(0, KVOL // UNROLL)
        def _(g):
            for j in range(UNROLL):
                k = g * UNROLL + j
                total = dot(grad_out[...], onehot[k], NN)
                high = total.astype(BF16)
                spread_hi[k] = high
                spread_lo[k] = (total - high.astype(F32)).astype(BF16)

    with jax.named_scope("table_grad"):
        total = None
        for k in range(0, KVOL, 4):
            n = min(4, KVOL - k)
            w = weight[k : k + n].reshape(n * SHARE, C)
            for part in (spread_hi, spread_lo):
                term = dot(w, part[k : k + n].reshape(n * SHARE, COLS), TN)
                total = term if total is None else total + term
        tg[...] = total.reshape(SUB, SHARE, COLS)

    def tg_copy(d):
        return copy("tg", d - 1, tg.at[y_peer(d)], tg_in.at[d - 1], (me, y_peer(d)))

    with jax.named_scope("tg_sends"):
        for d in range(1, SUB):
            tg_copy(d).start()

    with jax.named_scope("x_to_z_b"):
        x_to_z(1)

    def z_reduce(c):
        lo, hi = CHUNKS[c]

        @pl.loop(1, NZ)
        def _(d):
            z_copy(c, d).wait_recv()

        total = x_sum[c, own_tile(z)] + jnp.sum(decode(z_in[c], hi - lo), axis=0)
        scaled = total * (1.0 / math.sqrt(VOX * DOM))
        codes[c, core, x, own_tile(z)] = encode(scaled, hi - lo)

        @pl.loop(1, NZ)
        def _(d):
            gz_copy(c, d).start()

    def z_to_x(c):
        @pl.loop(1, NZ)
        def _(d):
            gz_arrival(c, d).wait_recv()

        for d in range(1, NX):
            gx_copy(c, d).start()

    def x_to_pair(c):
        for d in range(1, NX):
            gx_arrival(c, d).wait_recv()
        gpair_copy(c).start()

    with jax.named_scope("z_reduce_a"):
        z_reduce(0)

    with jax.named_scope("out_feats"):
        def out_step(g, acc):
            for j in range(UNROLL):
                acc = acc + dot(weight[g * UNROLL + j], picked[g * UNROLL + j], NT)
            return acc

        out_feats[...] = lax.fori_loop(0, KVOL // UNROLL, out_step, jnp.zeros((SHARE, VOX), F32)).astype(BF16)

    with jax.named_scope("z_reduce_b"):
        z_reduce(1)

    with jax.named_scope("tg_sum"):
        for d in range(1, SUB):
            tg_copy(d).wait_recv()
        mine_tg = tg[sub] + tg_in[0] + tg_in[1] + tg_in[2]
        tail = mine_tg[:, VOX:].T
        back_out[...] = jnp.concatenate([tail[:128], tail[128:]], axis=1).reshape(8, 16, 128)

    def back_copy(n):
        return copy("back", n, back_out.at[n], back_in.at[n], (wrap(me - HOPS[n]), sub))

    with jax.named_scope("back_sends"):
        for n in range(8):
            back_copy(n).start()

    with jax.named_scope("z_back"):
        z_to_x(0)
        z_to_x(1)
    with jax.named_scope("x_back"):
        x_to_pair(0)
        x_to_pair(1)

    with jax.named_scope("grad_feats"):
        for n in range(8):
            back_copy(n).wait_recv()
        back = back_in[...]
        back = jnp.concatenate([back[:, :, :SHARE][:, None], back[:, :, SHARE:][:, None]], axis=1)
        back = back.reshape(HALO, SHARE).T
        back_hi = back.astype(BF16)
        back_lo = (back - back_hi.astype(F32)).astype(BF16)
        grad_feats[...] = mine_tg[:, :VOX] + dot(back_hi, pick, NT) + dot(back_lo, pick, NT)

    with jax.named_scope("pair_back"):
        gpair_arrival(0).wait_recv()
        gpair_arrival(1).wait_recv()

    with jax.named_scope("drain"):
        for d in range(1, SUB):
            share_copy(d).wait_send()
            fwd_copy(d).wait_send()
            tg_copy(d).wait_send()
        for n in range(8):
            halo_copy(n).wait_send()
            back_copy(n).wait_send()
        for c in range(2):
            pair_copy(c).wait_send()
            gpair_copy(c).wait_send()
            for d in range(1, NX):
                x_copy(c, d).wait_send()
                gx_copy(c, d).wait_send()

            @pl.loop(1, NZ)
            def _(d):
                z_copy(c, d).wait_send()
                gz_copy(c, d).wait_send()


def finish(codes, out_in, feats_in, out_feats, grad_feats, grad_weight):
    out_feats[...] = out_in[...]
    grad_feats[...] = feats_in[...]
    for c, (lo, hi) in enumerate(CHUNKS):
        for cc in range(2):
            for xx in range(NX):
                values = decode(codes[c, cc, xx].reshape(16, 16, 128), hi - lo)
                r0, l0 = cc * 32 + (xx // 2) * 16, (xx % 2) * 128
                values = jnp.swapaxes(values, 0, 1)
                grad_weight[lo:hi, r0 : r0 + 16, l0 : l0 + 128] = values[: hi - lo]


def body(feats, weight, grad_out, neighbors, send_rows, send_counts):
    vmem = pl.BlockSpec(memory_space=pltpu.VMEM)
    out_feats, grad_feats, codes = pl.pallas_call(
        kernel,
        out_shape=(
            jax.ShapeDtypeStruct((SHARE, VOX), BF16),
            jax.ShapeDtypeStruct((SHARE, VOX), F32),
            jax.ShapeDtypeStruct((2, 2, NX, 256, 128), I16),
        ),
        in_specs=[vmem] * 6,
        out_specs=[vmem] * 3,
        scratch_shapes=[
            pltpu.VMEM((VOX, 128), jnp.int32),
            pltpu.VMEM((KVOL, VOX, COLS), BF16),
            pltpu.VMEM((KVOL, VOX, C), BF16),
            pltpu.VMEM((KVOL + 1, SHARE, COLS), BF16),
            pltpu.VMEM((KVOL + 1, SHARE, COLS), BF16),
            pltpu.VMEM((SUB, SHARE, VOX), BF16),
            pltpu.VMEM((8, 16, 128), BF16),
            pltpu.VMEM((8, 16, 128), BF16),
            pltpu.VMEM((SUB, 8, 16, 128), BF16),
            pltpu.VMEM((COLS, C), BF16),
            pltpu.VMEM((2, 2, NX, 256, 128), F32),
            pltpu.VMEM((2, NX, 256, 128), F32),
            pltpu.VMEM((2, NX, 256, 128), I16),
            pltpu.VMEM((2, NX - 1, 256, 128), I16),
            pltpu.VMEM((2, 256, 128), F32),
            pltpu.VMEM((2, 256, 128), I16),
            pltpu.VMEM((2, NZ - 1, 16, 128), I16),
            pltpu.VMEM((SUB, SHARE, COLS), F32),
            pltpu.VMEM((SUB - 1, SHARE, COLS), F32),
            pltpu.VMEM((8, 16, 128), F32),
            pltpu.VMEM((8, 16, 128), F32),
            pltpu.SemaphoreType.DMA((105,)),
            pltpu.SemaphoreType.DMA((105,)),
        ],
        compiler_params=pltpu.CompilerParams(
            collective_id=0, has_side_effects=True, vmem_limit_bytes=56 * 1024 * 1024
        ),
    )(feats, weight, grad_out, neighbors, send_rows, send_counts.T)
    return pl.pallas_call(
        finish,
        out_shape=(
            jax.ShapeDtypeStruct((SHARE, VOX), BF16),
            jax.ShapeDtypeStruct((SHARE, VOX), F32),
            jax.ShapeDtypeStruct((KVOL, SHARE, C), F32),
        ),
        in_specs=[vmem] * 3,
        out_specs=[vmem] * 3,
        compiler_params=pltpu.CompilerParams(vmem_limit_bytes=60 * 1024 * 1024),
    )(codes, out_feats, grad_feats)


def solution(mesh):
    in_specs = (
        P("sub", "dom"),
        P(None, "sub", None),
        P("sub", "dom"),
        P(None, "dom"),
        P("dom", None),
        P(),
    )
    out_specs = (P("sub", "dom"), P("sub", "dom"), P(None, "sub", None))
    return jax.shard_map(body, mesh=mesh, in_specs=in_specs, out_specs=out_specs, check_vma=False)
```

```python
import math

import jax
import jax.numpy as jnp
from jax import lax
from jax.experimental import pallas as pl
from jax.experimental.pallas import tpu as pltpu
from jax.sharding import PartitionSpec as P

C = 256
KVOL = 27
CAP = 32
SUB = 4
NX = 4
NZ = 16
DOM = 2 * NX * NZ
SHARE = C // SUB
VOX = 384
HALO = 8 * CAP
COLS = VOX + HALO
GRID_Y = 8
DIRECTIONS = ((-1, -1), (-1, 0), (-1, 1), (0, -1), (0, 1), (1, -1), (1, 0), (1, 1))
HOPS = tuple(dx * GRID_Y + dy for dx, dy in DIRECTIONS)
CHUNKS = ((0, 15), (15, 27))
UNROLL = 3
STEPS = 128.0
TOP = 32000.0
MESH = pl.DeviceIdType.MESH
F32 = jnp.float32
BF16 = jnp.bfloat16
I16 = jnp.int16


def dot(a, b, dims):
    return lax.dot_general(a, b, (dims, ((), ())), preferred_element_type=F32)


NN = ((1,), (0,))
NT = ((1,), (1,))
TN = ((0,), (0,))


def encode(tiles, n):
    row = lax.broadcasted_iota(jnp.int32, tiles.shape, tiles.ndim - 2)
    tiles = jnp.where(row < n, tiles, 0.0)
    top = jnp.max(jnp.abs(tiles), axis=-2, keepdims=True)
    level = jnp.ceil(jnp.log2(jnp.maximum(top, 1e-33)) * STEPS)
    codes = jnp.round(tiles * (jnp.exp2(level * (-1.0 / STEPS)) * TOP))
    return jnp.where(row == n, level, codes).astype(jnp.int32).astype(I16)


def decode(codes, n):
    values = codes.astype(jnp.int32).astype(F32)
    level = values[..., n : n + 1, :]
    return values * (jnp.exp2(level * (1.0 / STEPS)) * (1.0 / TOP))


def kernel(
    feats_hbm, weight_hbm, grad_out_hbm, neighbors_hbm, send_rows_hbm, send_counts_hbm,
    out_feats_hbm, grad_feats_hbm, codes_hbm,
    feats, weight, grad_out, neighbors, send_rows, send_counts, out_feats, grad_feats, codes,
    nbr_t, onehot, picked, spread_hi, spread_lo, share_all, halo_out, halo_in, halo_all,
    table, wg, pair_in, x_out, x_in, x_sum, z_out, z_in, tg, tg_in, back_out, back_in,
    send, recv, local,
):
    me = lax.axis_index("dom")
    sub = lax.axis_index("sub")
    core = lax.rem(me, 2)
    z = lax.rem(me // 2, NZ)
    x = me // (2 * NZ)

    def wrap(i):
        return lax.rem(i + DOM, DOM)

    def at(xx, zz, cc):
        return (xx * NZ + zz) * 2 + cc

    twin = at(x, z, 1 - core)

    def x_peer(d):
        return lax.rem(x + d, NX)

    def z_peer(d):
        return lax.rem(z + d, NZ)

    def y_peer(d):
        return lax.rem(sub + d, SUB)

    slots = {}

    def copy(name, index, src, dst, device):
        base = slots[name]
        return pltpu.make_async_remote_copy(
            src_ref=src, dst_ref=dst, send_sem=send.at[base + index], recv_sem=recv.at[base + index],
            device_id=device, device_id_type=MESH,
        )

    for base, name in enumerate(("share", "fwd", "tg")):
        slots[name] = 3 * base
    slots["halo"], slots["back"] = 9, 17
    slots["pair"], slots["gpair"] = 25, 27
    slots["x"], slots["gx"] = 29, 35
    slots["z"], slots["gz"] = 41, 73

    barrier = pltpu.get_barrier_semaphore()
    peers = [(me, y_peer(d)) for d in range(1, SUB)]
    peers += [(wrap(me + hop), sub) for hop in HOPS]
    peers += [(twin, sub)]
    peers += [(at(x_peer(d), z, core), sub) for d in range(1, NX)]
    with jax.named_scope("barrier_signals"):
        for peer in peers:
            pl.semaphore_signal(barrier, inc=1, device_id=peer, device_id_type=MESH)

        @pl.loop(1, NZ)
        def _(d):
            pl.semaphore_signal(barrier, inc=1, device_id=(at(x, z_peer(d), core), sub), device_id_type=MESH)

    def load(i):
        pairs = (
            (send_counts_hbm, send_counts), (send_rows_hbm, send_rows), (feats_hbm, feats),
            (neighbors_hbm, neighbors), (grad_out_hbm, grad_out), (weight_hbm, weight),
        )
        return pltpu.make_async_copy(pairs[i][0], pairs[i][1], local.at[i])

    def store(i):
        pairs = [(out_feats, out_feats_hbm), (grad_feats, grad_feats_hbm)]
        pairs += [(codes.at[c, half], codes_hbm.at[c, half]) for c in range(2) for half in (core, 1 - core)]
        return pltpu.make_async_copy(pairs[i][0], pairs[i][1], local.at[6 + i])

    with jax.named_scope("loads"):
        for i in range(6):
            load(i).start()

    with jax.named_scope("boundary_tiles"):
        for i in range(3):
            load(i).wait()
        lane = lax.broadcasted_iota(jnp.int32, (1, HALO), 1)
        mine = send_counts[...]
        mine = jnp.where(lax.broadcasted_iota(jnp.int32, (8, DOM), 1) == me, mine, 0).astype(F32)
        mine = jnp.sum(mine, axis=1, keepdims=True).astype(jnp.int32)
        count = jnp.zeros((1, HALO), jnp.int32)
        for n in range(8):
            count = jnp.where(lane // CAP == n, mine[n : n + 1, :], count)
        rows = jnp.where(lane % CAP < count, send_rows[...], -1)
        pick = (lax.broadcasted_iota(jnp.int32, (VOX, HALO), 0) == rows).astype(F32).astype(BF16)
        outgoing = dot(feats[...], pick, NN).T.reshape(8, 2, 16, SHARE)
        halo_out[...] = jnp.concatenate([outgoing[:, 0], outgoing[:, 1]], axis=-1).astype(BF16)

    with jax.named_scope("barrier_wait"):
        pl.semaphore_wait(barrier, len(peers) + NZ - 1)

    def share_copy(d):
        return copy("share", d - 1, feats, share_all.at[sub], (me, y_peer(d)))

    def halo_copy(n):
        return copy("halo", n, halo_out.at[n], halo_in.at[n], (wrap(me + HOPS[n]), sub))

    def fwd_copy(d):
        return copy("fwd", d - 1, halo_in, halo_all.at[sub], (me, y_peer(d)))

    with jax.named_scope("first_sends"):
        for n in range(8):
            halo_copy(n).start()
        for d in range(1, SUB):
            share_copy(d).start()
        share_all[sub] = feats[...]

    with jax.named_scope("transpose_maps"):
        for i in (3, 4, 5):
            load(i).wait()
        nbr_t[...] = jnp.concatenate(
            [neighbors[...], jnp.zeros((128 - KVOL, VOX), jnp.int32)], axis=0
        ).T
        col = lax.broadcasted_iota(jnp.int32, (1, COLS), 1)
        r = col - VOX
        slot = jnp.where(col < VOX, col, VOX + ((r % 128) // 16) * CAP + (r // 128) * 16 + r % 16)

    with jax.named_scope("onehot"):
        @pl.loop(0, KVOL // UNROLL)
        def _(g):
            now = nbr_t[...]
            nbr_t[...] = pltpu.roll(now, 128 - UNROLL, 1)
            for j in range(UNROLL):
                onehot[g * UNROLL + j] = (now[:, j : j + 1] == slot).astype(F32).astype(BF16)

    def gather_own(first, last):
        @pl.loop(first // UNROLL, last // UNROLL)
        def _(g):
            hot = onehot[pl.ds(g * UNROLL, UNROLL), :, 0:VOX].reshape(UNROLL * VOX, VOX)
            got = dot(hot, table[0:VOX], NN).astype(BF16)
            picked[pl.ds(g * UNROLL, UNROLL)] = got.reshape(UNROLL, VOX, C)

    with jax.named_scope("table_own"):
        for d in range(1, SUB):
            share_copy(d).wait_recv()
        table[0:VOX] = share_all[...].reshape(C, VOX).T
    with jax.named_scope("gather_own_a"):
        gather_own(0, 15)

    with jax.named_scope("halo_arrival"):
        for n in range(8):
            halo_copy(n).wait_recv()
        for d in range(1, SUB):
            fwd_copy(d).start()
        halo_all[sub] = halo_in[...]

    with jax.named_scope("gather_own_b"):
        gather_own(15, 27)

    with jax.named_scope("table_halo"):
        for d in range(1, SUB):
            fwd_copy(d).wait_recv()
        tiles = halo_all[...].reshape(SUB, 128, 128)
        for half in range(2):
            lanes = slice(half * SHARE, (half + 1) * SHARE)
            table[VOX + half * 128 : VOX + (half + 1) * 128] = jnp.concatenate(
                [tiles[s][:, lanes] for s in range(SUB)], axis=1
            )

    def pair_copy(c):
        return copy("pair", c, wg.at[c, 1 - core], pair_in.at[c], (twin, sub))

    def x_copy(c, d):
        return copy("x", 3 * c + d - 1, x_out.at[c, x_peer(d)], x_in.at[c, d - 1], (at(x_peer(d), z, core), sub))

    def own_tile(zz):
        return pl.ds(pl.multiple_of(zz * 16, 16), 16)

    def z_copy(c, d):
        return copy("z", 16 * c + d - 1, z_out.at[c, own_tile(z_peer(d))], z_in.at[c, d - 1], (at(x, z_peer(d), core), sub))

    def gz_copy(c, d):
        ref = codes.at[c, core, x, own_tile(z)]
        return copy("gz", 16 * c + d - 1, ref, ref, (at(x, z_peer(d), core), sub))

    def gz_arrival(c, d):
        ref = codes.at[c, core, x, own_tile(z_peer(NZ - d))]
        return copy("gz", 16 * c + d - 1, ref, ref, (at(x, z_peer(d), core), sub))

    def gx_copy(c, d):
        ref = codes.at[c, core, x]
        return copy("gx", 3 * c + d - 1, ref, ref, (at(x_peer(d), z, core), sub))

    def gx_arrival(c, d):
        ref = codes.at[c, core, x_peer(NX - d)]
        return copy("gx", 3 * c + d - 1, ref, ref, (at(x_peer(d), z, core), sub))

    def gpair_copy(c):
        ref = codes.at[c, core]
        return copy("gpair", c, ref, ref, (twin, sub))

    def gpair_arrival(c):
        ref = codes.at[c, 1 - core]
        return copy("gpair", c, ref, ref, (twin, sub))

    def gather(c, first, last):
        lo = CHUNKS[c][0]

        @pl.loop(first // UNROLL, last // UNROLL)
        def _(g):
            k0 = g * UNROLL
            hot = onehot[pl.ds(k0, UNROLL), :, VOX:COLS].reshape(UNROLL * VOX, HALO)
            got = dot(hot, table[VOX:COLS], NN).astype(BF16).reshape(UNROLL, VOX, C)
            got = got + picked[pl.ds(k0, UNROLL)]
            picked[pl.ds(k0, UNROLL)] = got
            for j in range(UNROLL):
                fresh = dot(grad_out[...], got[j], NN)
                for cc in range(2):
                    for xx in range(NX):
                        r0, l0 = cc * 32 + (xx // 2) * 16, (xx % 2) * 128
                        wg[c, cc, xx, pl.ds(k0 + j - lo, 16, stride=16), :] = fresh[r0 : r0 + 16, l0 : l0 + 128]

    def pair_to_x(c):
        lo, hi = CHUNKS[c]
        pair_copy(c).wait_recv()
        for xx in range(NX):
            both = wg[c, core, xx] + pair_in[c, xx]
            x_out[c, xx] = encode(both.reshape(16, 16, 128), hi - lo).reshape(256, 128)
        for d in range(1, NX):
            x_copy(c, d).start()

    def x_to_z(c):
        lo, hi = CHUNKS[c]
        for d in range(1, NX):
            x_copy(c, d).wait_recv()
        total = (wg[c, core, x] + pair_in[c, x]).reshape(16, 16, 128)
        for d in range(1, NX):
            total = total + decode(x_in[c, d - 1].reshape(16, 16, 128), hi - lo)
        x_sum[c] = total.reshape(256, 128)
        z_out[c] = encode(total, hi - lo).reshape(256, 128)

        @pl.loop(1, NZ)
        def _(d):
            z_copy(c, d).start()

    with jax.named_scope("wg_rows"):
        for c, (lo, hi) in enumerate(CHUNKS):
            for row in range(hi - lo, 16):
                for cc in range(2):
                    for xx in range(NX):
                        wg[c, cc, xx, pl.ds(row, 16, stride=16), :] = jnp.zeros((16, 128), F32)

    with jax.named_scope("gather_a"):
        gather(0, 0, 15)
    with jax.named_scope("pair_a"):
        pair_copy(0).start()
    with jax.named_scope("gather_b"):
        gather(1, 15, 21)
    with jax.named_scope("pair_to_x_a"):
        pair_to_x(0)
    with jax.named_scope("gather_c"):
        gather(1, 21, 27)
    with jax.named_scope("pair_b"):
        pair_copy(1).start()

    with jax.named_scope("pair_to_x_b"):
        pair_to_x(1)

    with jax.named_scope("spread"):
        @pl.loop(0, KVOL // UNROLL)
        def _(g):
            for j in range(UNROLL):
                k = g * UNROLL + j
                total = dot(grad_out[...], onehot[k], NN)
                high = total.astype(BF16)
                spread_hi[k] = high
                spread_lo[k] = (total - high.astype(F32)).astype(BF16)

    with jax.named_scope("x_to_z_a"):
        x_to_z(0)

    with jax.named_scope("table_grad"):
        total = None
        for k in range(0, KVOL, 4):
            n = min(4, KVOL - k)
            w = weight[k : k + n].reshape(n * SHARE, C)
            for part in (spread_hi, spread_lo):
                term = dot(w, part[k : k + n].reshape(n * SHARE, COLS), TN)
                total = term if total is None else total + term
        tg[...] = total.reshape(SUB, SHARE, COLS)

    def tg_copy(d):
        return copy("tg", d - 1, tg.at[y_peer(d)], tg_in.at[d - 1], (me, y_peer(d)))

    with jax.named_scope("tg_sends"):
        for d in range(1, SUB):
            tg_copy(d).start()

    with jax.named_scope("x_to_z_b"):
        x_to_z(1)

    def z_reduce(c):
        lo, hi = CHUNKS[c]

        @pl.loop(1, NZ)
        def _(d):
            z_copy(c, d).wait_recv()

        total = x_sum[c, own_tile(z)] + jnp.sum(decode(z_in[c], hi - lo), axis=0)
        scaled = total * (1.0 / math.sqrt(VOX * DOM))
        codes[c, core, x, own_tile(z)] = encode(scaled, hi - lo)

        @pl.loop(1, NZ)
        def _(d):
            gz_copy(c, d).start()

    def z_to_x(c):
        @pl.loop(1, NZ)
        def _(d):
            gz_arrival(c, d).wait_recv()

        for d in range(1, NX):
            gx_copy(c, d).start()

    def x_to_pair(c):
        for d in range(1, NX):
            gx_arrival(c, d).wait_recv()
        gpair_copy(c).start()
        store(2 + 2 * c).start()

    with jax.named_scope("z_reduce_a"):
        z_reduce(0)

    with jax.named_scope("out_feats"):
        def out_step(g, acc):
            for j in range(UNROLL):
                acc = acc + dot(weight[g * UNROLL + j], picked[g * UNROLL + j], NT)
            return acc

        out_feats[...] = lax.fori_loop(0, KVOL // UNROLL, out_step, jnp.zeros((SHARE, VOX), F32)).astype(BF16)
        store(0).start()

    with jax.named_scope("z_reduce_b"):
        z_reduce(1)

    with jax.named_scope("tg_sum"):
        for d in range(1, SUB):
            tg_copy(d).wait_recv()
        mine_tg = tg[sub] + tg_in[0] + tg_in[1] + tg_in[2]
        tail = mine_tg[:, VOX:].T
        back_out[...] = jnp.concatenate([tail[:128], tail[128:]], axis=1).reshape(8, 16, 128)

    def back_copy(n):
        return copy("back", n, back_out.at[n], back_in.at[n], (wrap(me - HOPS[n]), sub))

    with jax.named_scope("back_sends"):
        for n in range(8):
            back_copy(n).start()

    with jax.named_scope("z_back"):
        z_to_x(0)
        z_to_x(1)
    with jax.named_scope("x_back"):
        x_to_pair(0)
        x_to_pair(1)

    with jax.named_scope("grad_feats"):
        for n in range(8):
            back_copy(n).wait_recv()
        back = back_in[...]
        back = jnp.concatenate([back[:, :, :SHARE][:, None], back[:, :, SHARE:][:, None]], axis=1)
        back = back.reshape(HALO, SHARE).T
        back_hi = back.astype(BF16)
        back_lo = (back - back_hi.astype(F32)).astype(BF16)
        grad_feats[...] = mine_tg[:, :VOX] + dot(back_hi, pick, NT) + dot(back_lo, pick, NT)
        store(1).start()

    with jax.named_scope("pair_back"):
        for c in range(2):
            gpair_arrival(c).wait_recv()
            store(3 + 2 * c).start()

    with jax.named_scope("drain"):
        for d in range(1, SUB):
            share_copy(d).wait_send()
            fwd_copy(d).wait_send()
            tg_copy(d).wait_send()
        for n in range(8):
            halo_copy(n).wait_send()
            back_copy(n).wait_send()
        for c in range(2):
            pair_copy(c).wait_send()
            gpair_copy(c).wait_send()
            for d in range(1, NX):
                x_copy(c, d).wait_send()
                gx_copy(c, d).wait_send()

            @pl.loop(1, NZ)
            def _(d):
                z_copy(c, d).wait_send()
                gz_copy(c, d).wait_send()
    with jax.named_scope("stores"):
        for i in range(6):
            store(i).wait()


def finish(codes_hbm, out_in, feats_in, out_feats, grad_feats, grad_weight_hbm, codes, grad_weight, arrive, leave):
    parts = [(c, half) for c in range(2) for half in range(2)]

    def load(i):
        c, half = parts[i]
        return pltpu.make_async_copy(codes_hbm.at[c, half], codes.at[c, half], arrive.at[i])

    def store(i):
        (lo, hi), r0 = CHUNKS[parts[i][0]], 32 * parts[i][1]
        where = (slice(lo, hi), slice(r0, r0 + 32))
        return pltpu.make_async_copy(grad_weight.at[where], grad_weight_hbm.at[where], leave.at[i])

    through = [
        pltpu.make_async_copy(out_in, out_feats, leave.at[4]),
        pltpu.make_async_copy(feats_in, grad_feats, leave.at[5]),
    ]
    for i in range(4):
        load(i).start()
    for one in through:
        one.start()
    for i, (c, half) in enumerate(parts):
        lo, hi = CHUNKS[c]
        load(i).wait()
        for xx in range(NX):
            values = decode(codes[c, half, xx].reshape(16, 16, 128), hi - lo)
            r0, l0 = half * 32 + (xx // 2) * 16, (xx % 2) * 128
            values = jnp.swapaxes(values, 0, 1)
            grad_weight[lo:hi, r0 : r0 + 16, l0 : l0 + 128] = values[: hi - lo]
        store(i).start()
    for i in range(4):
        store(i).wait()
    for one in through:
        one.wait()


def body(feats, weight, grad_out, neighbors, send_rows, send_counts):
    hbm = pl.BlockSpec(memory_space=pltpu.HBM)
    out_feats, grad_feats, codes = pl.pallas_call(
        kernel,
        out_shape=(
            jax.ShapeDtypeStruct((SHARE, VOX), BF16),
            jax.ShapeDtypeStruct((SHARE, VOX), F32),
            jax.ShapeDtypeStruct((2, 2, NX, 256, 128), I16),
        ),
        in_specs=[hbm] * 6,
        out_specs=[hbm] * 3,
        scratch_shapes=[
            pltpu.VMEM((SHARE, VOX), BF16),
            pltpu.VMEM((KVOL, SHARE, C), BF16),
            pltpu.VMEM((SHARE, VOX), BF16),
            pltpu.VMEM((KVOL, VOX), jnp.int32),
            pltpu.VMEM((1, HALO), jnp.int32),
            pltpu.VMEM((8, DOM), jnp.int32),
            pltpu.VMEM((SHARE, VOX), BF16),
            pltpu.VMEM((SHARE, VOX), F32),
            pltpu.VMEM((2, 2, NX, 256, 128), I16),
            pltpu.VMEM((VOX, 128), jnp.int32),
            pltpu.VMEM((KVOL, VOX, COLS), BF16),
            pltpu.VMEM((KVOL, VOX, C), BF16),
            pltpu.VMEM((KVOL + 1, SHARE, COLS), BF16),
            pltpu.VMEM((KVOL + 1, SHARE, COLS), BF16),
            pltpu.VMEM((SUB, SHARE, VOX), BF16),
            pltpu.VMEM((8, 16, 128), BF16),
            pltpu.VMEM((8, 16, 128), BF16),
            pltpu.VMEM((SUB, 8, 16, 128), BF16),
            pltpu.VMEM((COLS, C), BF16),
            pltpu.VMEM((2, 2, NX, 256, 128), F32),
            pltpu.VMEM((2, NX, 256, 128), F32),
            pltpu.VMEM((2, NX, 256, 128), I16),
            pltpu.VMEM((2, NX - 1, 256, 128), I16),
            pltpu.VMEM((2, 256, 128), F32),
            pltpu.VMEM((2, 256, 128), I16),
            pltpu.VMEM((2, NZ - 1, 16, 128), I16),
            pltpu.VMEM((SUB, SHARE, COLS), F32),
            pltpu.VMEM((SUB - 1, SHARE, COLS), F32),
            pltpu.VMEM((8, 16, 128), F32),
            pltpu.VMEM((8, 16, 128), F32),
            pltpu.SemaphoreType.DMA((105,)),
            pltpu.SemaphoreType.DMA((105,)),
            pltpu.SemaphoreType.DMA((12,)),
        ],
        compiler_params=pltpu.CompilerParams(
            collective_id=0, has_side_effects=True, vmem_limit_bytes=56 * 1024 * 1024
        ),
    )(feats, weight, grad_out, neighbors, send_rows, send_counts.T)
    return pl.pallas_call(
        finish,
        out_shape=(
            jax.ShapeDtypeStruct((SHARE, VOX), BF16),
            jax.ShapeDtypeStruct((SHARE, VOX), F32),
            jax.ShapeDtypeStruct((KVOL, SHARE, C), F32),
        ),
        in_specs=[hbm] * 3,
        out_specs=[hbm] * 3,
        scratch_shapes=[
            pltpu.VMEM((2, 2, NX, 256, 128), I16),
            pltpu.VMEM((KVOL, SHARE, C), F32),
            pltpu.SemaphoreType.DMA((4,)),
            pltpu.SemaphoreType.DMA((6,)),
        ],
        compiler_params=pltpu.CompilerParams(vmem_limit_bytes=60 * 1024 * 1024),
    )(codes, out_feats, grad_feats)


def solution(mesh):
    in_specs = (
        P("sub", "dom"),
        P(None, "sub", None),
        P("sub", "dom"),
        P(None, "dom"),
        P("dom", None),
        P(),
    )
    out_specs = (P("sub", "dom"), P("sub", "dom"), P(None, "sub", None))
    return jax.shard_map(body, mesh=mesh, in_specs=in_specs, out_specs=out_specs, check_vma=False)
```

```python
import math

import jax
import jax.numpy as jnp
from jax import lax
from jax.experimental import pallas as pl
from jax.experimental.pallas import tpu as pltpu
from jax.sharding import PartitionSpec as P

C = 256
KVOL = 27
CAP = 32
SUB = 4
NX = 4
NZ = 16
DOM = 2 * NX * NZ
SHARE = C // SUB
VOX = 384
HALO = 8 * CAP
COLS = VOX + HALO
GRID_Y = 8
DIRECTIONS = ((-1, -1), (-1, 0), (-1, 1), (0, -1), (0, 1), (1, -1), (1, 0), (1, 1))
HOPS = tuple(dx * GRID_Y + dy for dx, dy in DIRECTIONS)
CHUNKS = ((0, 15), (15, 27))
UNROLL = 3
STEPS = 128.0
TOP = 32000.0
MESH = pl.DeviceIdType.MESH
F32 = jnp.float32
BF16 = jnp.bfloat16
I16 = jnp.int16


def dot(a, b, dims):
    return lax.dot_general(a, b, (dims, ((), ())), preferred_element_type=F32)


NN = ((1,), (0,))
NT = ((1,), (1,))
TN = ((0,), (0,))


def encode(tiles, n):
    row = lax.broadcasted_iota(jnp.int32, tiles.shape, tiles.ndim - 2)
    tiles = jnp.where(row < n, tiles, 0.0)
    top = jnp.max(jnp.abs(tiles), axis=-2, keepdims=True)
    level = jnp.ceil(jnp.log2(jnp.maximum(top, 1e-33)) * STEPS)
    codes = jnp.round(tiles * (jnp.exp2(level * (-1.0 / STEPS)) * TOP))
    return jnp.where(row == n, level, codes).astype(jnp.int32).astype(I16)


def decode(codes, n):
    values = codes.astype(jnp.int32).astype(F32)
    level = values[..., n : n + 1, :]
    return values * (jnp.exp2(level * (1.0 / STEPS)) * (1.0 / TOP))


def kernel(
    feats_hbm, weight_hbm, grad_out_hbm, neighbors_hbm, send_rows_hbm, send_counts_hbm,
    out_feats_hbm, grad_feats_hbm, codes_hbm,
    feats, weight, grad_out, neighbors, send_rows, send_counts, out_feats, grad_feats, codes,
    nbr_t, onehot, picked, spread_hi, spread_lo, share_all, halo_out, halo_in, halo_all,
    table, wg, pair_in, x_out, x_in, x_sum, z_out, z_in, tg, tg_in, back_out, back_in,
    send, recv, local,
):
    me = lax.axis_index("dom")
    sub = lax.axis_index("sub")
    core = lax.rem(me, 2)
    z = lax.rem(me // 2, NZ)
    x = me // (2 * NZ)

    def wrap(i):
        return lax.rem(i + DOM, DOM)

    def at(xx, zz, cc):
        return (xx * NZ + zz) * 2 + cc

    twin = at(x, z, 1 - core)

    def x_peer(d):
        return lax.rem(x + d, NX)

    def z_peer(d):
        return lax.rem(z + d, NZ)

    def far_first(i):
        return NZ // 2 + ((i + 1) // 2) * (2 * lax.rem(i, 2) - 1)

    def y_peer(d):
        return lax.rem(sub + d, SUB)

    slots = {}

    def copy(name, index, src, dst, device):
        base = slots[name]
        return pltpu.make_async_remote_copy(
            src_ref=src, dst_ref=dst, send_sem=send.at[base + index], recv_sem=recv.at[base + index],
            device_id=device, device_id_type=MESH,
        )

    for base, name in enumerate(("share", "fwd", "tg")):
        slots[name] = 3 * base
    slots["halo"], slots["back"] = 9, 17
    slots["pair"], slots["gpair"] = 25, 27
    slots["x"], slots["gx"] = 29, 35
    slots["z"], slots["gz"] = 41, 73

    barrier = pltpu.get_barrier_semaphore()
    peers = [(me, y_peer(d)) for d in range(1, SUB)]
    peers += [(wrap(me + hop), sub) for hop in HOPS]
    peers += [(twin, sub)]
    peers += [(at(x_peer(d), z, core), sub) for d in range(1, NX)]
    def load(i):
        pairs = (
            (send_counts_hbm, send_counts), (send_rows_hbm, send_rows), (feats_hbm, feats),
            (neighbors_hbm, neighbors), (grad_out_hbm, grad_out), (weight_hbm, weight),
        )
        return pltpu.make_async_copy(pairs[i][0], pairs[i][1], local.at[i])

    def store(i):
        pairs = [(out_feats, out_feats_hbm), (grad_feats, grad_feats_hbm)]
        pairs += [(codes.at[c, half], codes_hbm.at[c, half]) for c in range(2) for half in (core, 1 - core)]
        return pltpu.make_async_copy(pairs[i][0], pairs[i][1], local.at[6 + i])

    with jax.named_scope("loads_first"):
        for i in range(3):
            load(i).start()

    with jax.named_scope("barrier_signals"):
        @pl.loop(0, NZ - 1)
        def _(i):
            peer = (at(x, z_peer(far_first(i)), core), sub)
            pl.semaphore_signal(barrier, inc=1, device_id=peer, device_id_type=MESH)

        for peer in peers:
            pl.semaphore_signal(barrier, inc=1, device_id=peer, device_id_type=MESH)

    with jax.named_scope("loads"):
        for i in range(3, 6):
            load(i).start()

    with jax.named_scope("boundary_tiles"):
        for i in range(3):
            load(i).wait()
        lane = lax.broadcasted_iota(jnp.int32, (1, HALO), 1)
        mine = send_counts[...]
        mine = jnp.where(lax.broadcasted_iota(jnp.int32, (8, DOM), 1) == me, mine, 0).astype(F32)
        mine = jnp.sum(mine, axis=1, keepdims=True).astype(jnp.int32)
        count = jnp.zeros((1, HALO), jnp.int32)
        for n in range(8):
            count = jnp.where(lane // CAP == n, mine[n : n + 1, :], count)
        rows = jnp.where(lane % CAP < count, send_rows[...], -1)
        pick = (lax.broadcasted_iota(jnp.int32, (VOX, HALO), 0) == rows).astype(F32).astype(BF16)
        outgoing = dot(feats[...], pick, NN).T.reshape(8, 2, 16, SHARE)
        halo_out[...] = jnp.concatenate([outgoing[:, 0], outgoing[:, 1]], axis=-1).astype(BF16)

    with jax.named_scope("barrier_wait"):
        pl.semaphore_wait(barrier, len(peers) + NZ - 1)

    def share_copy(d):
        return copy("share", d - 1, feats, share_all.at[sub], (me, y_peer(d)))

    def halo_copy(n):
        return copy("halo", n, halo_out.at[n], halo_in.at[n], (wrap(me + HOPS[n]), sub))

    def fwd_copy(d):
        return copy("fwd", d - 1, halo_in, halo_all.at[sub], (me, y_peer(d)))

    with jax.named_scope("first_sends"):
        for n in range(8):
            halo_copy(n).start()
        for d in range(1, SUB):
            share_copy(d).start()
        share_all[sub] = feats[...]

    with jax.named_scope("transpose_maps"):
        for i in (3, 4, 5):
            load(i).wait()
        nbr_t[...] = jnp.concatenate(
            [neighbors[...], jnp.zeros((128 - KVOL, VOX), jnp.int32)], axis=0
        ).T
        col = lax.broadcasted_iota(jnp.int32, (1, COLS), 1)
        r = col - VOX
        slot = jnp.where(col < VOX, col, VOX + ((r % 128) // 16) * CAP + (r // 128) * 16 + r % 16)

    with jax.named_scope("onehot"):
        @pl.loop(0, KVOL // UNROLL)
        def _(g):
            now = nbr_t[...]
            nbr_t[...] = pltpu.roll(now, 128 - UNROLL, 1)
            for j in range(UNROLL):
                onehot[g * UNROLL + j] = (now[:, j : j + 1] == slot).astype(F32).astype(BF16)

    def gather_own(first, last):
        @pl.loop(first // UNROLL, last // UNROLL)
        def _(g):
            hot = onehot[pl.ds(g * UNROLL, UNROLL), :, 0:VOX].reshape(UNROLL * VOX, VOX)
            got = dot(hot, table[0:VOX], NN).astype(BF16)
            picked[pl.ds(g * UNROLL, UNROLL)] = got.reshape(UNROLL, VOX, C)

    with jax.named_scope("table_own"):
        for d in range(1, SUB):
            share_copy(d).wait_recv()
        table[0:VOX] = share_all[...].reshape(C, VOX).T
    with jax.named_scope("gather_own_a"):
        gather_own(0, 15)

    with jax.named_scope("halo_arrival"):
        for n in range(8):
            halo_copy(n).wait_recv()
        for d in range(1, SUB):
            fwd_copy(d).start()
        halo_all[sub] = halo_in[...]

    with jax.named_scope("gather_own_b"):
        gather_own(15, 27)

    with jax.named_scope("table_halo"):
        for d in range(1, SUB):
            fwd_copy(d).wait_recv()
        tiles = halo_all[...].reshape(SUB, 128, 128)
        for half in range(2):
            lanes = slice(half * SHARE, (half + 1) * SHARE)
            table[VOX + half * 128 : VOX + (half + 1) * 128] = jnp.concatenate(
                [tiles[s][:, lanes] for s in range(SUB)], axis=1
            )

    def pair_copy(c):
        return copy("pair", c, wg.at[c, 1 - core], pair_in.at[c], (twin, sub))

    def x_copy(c, d):
        return copy("x", 3 * c + d - 1, x_out.at[c, x_peer(d)], x_in.at[c, d - 1], (at(x_peer(d), z, core), sub))

    def own_tile(zz):
        return pl.ds(pl.multiple_of(zz * 16, 16), 16)

    def z_copy(c, d):
        return copy("z", 16 * c + d - 1, z_out.at[c, own_tile(z_peer(d))], z_in.at[c, d - 1], (at(x, z_peer(d), core), sub))

    def gz_copy(c, d):
        ref = codes.at[c, core, x, own_tile(z)]
        return copy("gz", 16 * c + d - 1, ref, ref, (at(x, z_peer(d), core), sub))

    def gz_arrival(c, d):
        ref = codes.at[c, core, x, own_tile(z_peer(NZ - d))]
        return copy("gz", 16 * c + d - 1, ref, ref, (at(x, z_peer(d), core), sub))

    def gx_copy(c, d):
        ref = codes.at[c, core, x]
        return copy("gx", 3 * c + d - 1, ref, ref, (at(x_peer(d), z, core), sub))

    def gx_arrival(c, d):
        ref = codes.at[c, core, x_peer(NX - d)]
        return copy("gx", 3 * c + d - 1, ref, ref, (at(x_peer(d), z, core), sub))

    def gpair_copy(c):
        ref = codes.at[c, core]
        return copy("gpair", c, ref, ref, (twin, sub))

    def gpair_arrival(c):
        ref = codes.at[c, 1 - core]
        return copy("gpair", c, ref, ref, (twin, sub))

    def gather(c, first, last):
        lo = CHUNKS[c][0]

        @pl.loop(first // UNROLL, last // UNROLL)
        def _(g):
            k0 = g * UNROLL
            hot = onehot[pl.ds(k0, UNROLL), :, VOX:COLS].reshape(UNROLL * VOX, HALO)
            got = dot(hot, table[VOX:COLS], NN).astype(BF16).reshape(UNROLL, VOX, C)
            got = got + picked[pl.ds(k0, UNROLL)]
            picked[pl.ds(k0, UNROLL)] = got
            for j in range(UNROLL):
                fresh = dot(grad_out[...], got[j], NN)
                for cc in range(2):
                    for xx in range(NX):
                        r0, l0 = cc * 32 + (xx // 2) * 16, (xx % 2) * 128
                        wg[c, cc, xx, pl.ds(k0 + j - lo, 16, stride=16), :] = fresh[r0 : r0 + 16, l0 : l0 + 128]

    def pair_to_x(c):
        lo, hi = CHUNKS[c]
        pair_copy(c).wait_recv()
        for xx in range(NX):
            both = wg[c, core, xx] + pair_in[c, xx]
            x_out[c, xx] = encode(both.reshape(16, 16, 128), hi - lo).reshape(256, 128)
        for d in (2, 1, 3):
            x_copy(c, d).start()

    def x_to_z(c):
        lo, hi = CHUNKS[c]
        for d in range(1, NX):
            x_copy(c, d).wait_recv()
        total = (wg[c, core, x] + pair_in[c, x]).reshape(16, 16, 128)
        for d in range(1, NX):
            total = total + decode(x_in[c, d - 1].reshape(16, 16, 128), hi - lo)
        x_sum[c] = total.reshape(256, 128)
        z_out[c] = encode(total, hi - lo).reshape(256, 128)

        @pl.loop(0, NZ - 1)
        def _(i):
            z_copy(c, far_first(i)).start()

    with jax.named_scope("wg_rows"):
        for c, (lo, hi) in enumerate(CHUNKS):
            for row in range(hi - lo, 16):
                for cc in range(2):
                    for xx in range(NX):
                        wg[c, cc, xx, pl.ds(row, 16, stride=16), :] = jnp.zeros((16, 128), F32)

    with jax.named_scope("gather_a"):
        gather(0, 0, 15)
    with jax.named_scope("pair_a"):
        pair_copy(0).start()
    with jax.named_scope("gather_b"):
        gather(1, 15, 21)
    with jax.named_scope("pair_to_x_a"):
        pair_to_x(0)
    with jax.named_scope("gather_c"):
        gather(1, 21, 27)
    with jax.named_scope("pair_b"):
        pair_copy(1).start()

    def spread(first, last):
        @pl.loop(first, last)
        def _(g):
            for j in range(UNROLL):
                k = g * UNROLL + j
                total = dot(grad_out[...], onehot[k], NN)
                high = total.astype(BF16)
                spread_hi[k] = high
                spread_lo[k] = (total - high.astype(F32)).astype(BF16)

    with jax.named_scope("spread_a"):
        spread(0, 5)
    with jax.named_scope("pair_to_x_b"):
        pair_to_x(1)
    with jax.named_scope("spread_b"):
        spread(5, 9)

    with jax.named_scope("x_to_z_a"):
        x_to_z(0)

    with jax.named_scope("table_grad"):
        total = None
        for k in range(0, KVOL, 4):
            n = min(4, KVOL - k)
            w = weight[k : k + n].reshape(n * SHARE, C)
            for part in (spread_hi, spread_lo):
                term = dot(w, part[k : k + n].reshape(n * SHARE, COLS), TN)
                total = term if total is None else total + term
        tg[...] = total.reshape(SUB, SHARE, COLS)

    def tg_copy(d):
        return copy("tg", d - 1, tg.at[y_peer(d)], tg_in.at[d - 1], (me, y_peer(d)))

    with jax.named_scope("tg_sends"):
        for d in range(1, SUB):
            tg_copy(d).start()

    with jax.named_scope("x_to_z_b"):
        x_to_z(1)

    def z_reduce(c):
        lo, hi = CHUNKS[c]

        @pl.loop(1, NZ)
        def _(d):
            z_copy(c, d).wait_recv()

        total = x_sum[c, own_tile(z)] + jnp.sum(decode(z_in[c], hi - lo), axis=0)
        scaled = total * (1.0 / math.sqrt(VOX * DOM))
        codes[c, core, x, own_tile(z)] = encode(scaled, hi - lo)

        @pl.loop(0, NZ - 1)
        def _(i):
            gz_copy(c, far_first(i)).start()

    def z_to_x(c):
        @pl.loop(1, NZ)
        def _(d):
            gz_arrival(c, d).wait_recv()

        for d in (2, 1, 3):
            gx_copy(c, d).start()

    def x_to_pair(c):
        for d in range(1, NX):
            gx_arrival(c, d).wait_recv()
        gpair_copy(c).start()
        store(2 + 2 * c).start()

    with jax.named_scope("z_reduce_a"):
        z_reduce(0)

    with jax.named_scope("tg_sum"):
        for d in range(1, SUB):
            tg_copy(d).wait_recv()
        mine_tg = tg[sub] + tg_in[0] + tg_in[1] + tg_in[2]
        tail = mine_tg[:, VOX:].T
        back_out[...] = jnp.concatenate([tail[:128], tail[128:]], axis=1).reshape(8, 16, 128)

    def back_copy(n):
        return copy("back", n, back_out.at[n], back_in.at[n], (wrap(me - HOPS[n]), sub))

    with jax.named_scope("back_sends"):
        for n in range(8):
            back_copy(n).start()

    with jax.named_scope("out_feats"):
        def out_step(g, acc):
            for j in range(UNROLL):
                acc = acc + dot(weight[g * UNROLL + j], picked[g * UNROLL + j], NT)
            return acc

        out_feats[...] = lax.fori_loop(0, KVOL // UNROLL, out_step, jnp.zeros((SHARE, VOX), F32)).astype(BF16)
        store(0).start()

    with jax.named_scope("z_reduce_b"):
        z_reduce(1)

    with jax.named_scope("z_back"):
        z_to_x(0)
        z_to_x(1)
    with jax.named_scope("x_back"):
        x_to_pair(0)
        x_to_pair(1)

    with jax.named_scope("grad_feats"):
        for n in range(8):
            back_copy(n).wait_recv()
        back = back_in[...]
        back = jnp.concatenate([back[:, :, :SHARE][:, None], back[:, :, SHARE:][:, None]], axis=1)
        back = back.reshape(HALO, SHARE).T
        back_hi = back.astype(BF16)
        back_lo = (back - back_hi.astype(F32)).astype(BF16)
        grad_feats[...] = mine_tg[:, :VOX] + dot(back_hi, pick, NT) + dot(back_lo, pick, NT)
        store(1).start()

    with jax.named_scope("pair_back"):
        for c in range(2):
            gpair_arrival(c).wait_recv()
            store(3 + 2 * c).start()

    with jax.named_scope("drain"):
        for d in range(1, SUB):
            share_copy(d).wait_send()
            fwd_copy(d).wait_send()
            tg_copy(d).wait_send()
        for n in range(8):
            halo_copy(n).wait_send()
            back_copy(n).wait_send()
        for c in range(2):
            pair_copy(c).wait_send()
            gpair_copy(c).wait_send()
            for d in range(1, NX):
                x_copy(c, d).wait_send()
                gx_copy(c, d).wait_send()

            @pl.loop(1, NZ)
            def _(d):
                z_copy(c, d).wait_send()
                gz_copy(c, d).wait_send()
    with jax.named_scope("stores"):
        for i in range(6):
            store(i).wait()


def finish(codes, out_in, feats_in, out_feats, grad_feats, grad_weight):
    out_feats[...] = out_in[...]
    grad_feats[...] = feats_in[...]
    for c, (lo, hi) in enumerate(CHUNKS):
        for cc in range(2):
            for xx in range(NX):
                values = decode(codes[c, cc, xx].reshape(16, 16, 128), hi - lo)
                r0, l0 = cc * 32 + (xx // 2) * 16, (xx % 2) * 128
                values = jnp.swapaxes(values, 0, 1)
                grad_weight[lo:hi, r0 : r0 + 16, l0 : l0 + 128] = values[: hi - lo]


def body(feats, weight, grad_out, neighbors, send_rows, send_counts):
    hbm = pl.BlockSpec(memory_space=pltpu.HBM)
    vmem = pl.BlockSpec(memory_space=pltpu.VMEM)
    out_feats, grad_feats, codes = pl.pallas_call(
        kernel,
        out_shape=(
            jax.ShapeDtypeStruct((SHARE, VOX), BF16),
            jax.ShapeDtypeStruct((SHARE, VOX), F32),
            jax.ShapeDtypeStruct((2, 2, NX, 256, 128), I16),
        ),
        in_specs=[hbm] * 6,
        out_specs=[hbm] * 3,
        scratch_shapes=[
            pltpu.VMEM((SHARE, VOX), BF16),
            pltpu.VMEM((KVOL, SHARE, C), BF16),
            pltpu.VMEM((SHARE, VOX), BF16),
            pltpu.VMEM((KVOL, VOX), jnp.int32),
            pltpu.VMEM((1, HALO), jnp.int32),
            pltpu.VMEM((8, DOM), jnp.int32),
            pltpu.VMEM((SHARE, VOX), BF16),
            pltpu.VMEM((SHARE, VOX), F32),
            pltpu.VMEM((2, 2, NX, 256, 128), I16),
            pltpu.VMEM((VOX, 128), jnp.int32),
            pltpu.VMEM((KVOL, VOX, COLS), BF16),
            pltpu.VMEM((KVOL, VOX, C), BF16),
            pltpu.VMEM((KVOL + 1, SHARE, COLS), BF16),
            pltpu.VMEM((KVOL + 1, SHARE, COLS), BF16),
            pltpu.VMEM((SUB, SHARE, VOX), BF16),
            pltpu.VMEM((8, 16, 128), BF16),
            pltpu.VMEM((8, 16, 128), BF16),
            pltpu.VMEM((SUB, 8, 16, 128), BF16),
            pltpu.VMEM((COLS, C), BF16),
            pltpu.VMEM((2, 2, NX, 256, 128), F32),
            pltpu.VMEM((2, NX, 256, 128), F32),
            pltpu.VMEM((2, NX, 256, 128), I16),
            pltpu.VMEM((2, NX - 1, 256, 128), I16),
            pltpu.VMEM((2, 256, 128), F32),
            pltpu.VMEM((2, 256, 128), I16),
            pltpu.VMEM((2, NZ - 1, 16, 128), I16),
            pltpu.VMEM((SUB, SHARE, COLS), F32),
            pltpu.VMEM((SUB - 1, SHARE, COLS), F32),
            pltpu.VMEM((8, 16, 128), F32),
            pltpu.VMEM((8, 16, 128), F32),
            pltpu.SemaphoreType.DMA((105,)),
            pltpu.SemaphoreType.DMA((105,)),
            pltpu.SemaphoreType.DMA((12,)),
        ],
        compiler_params=pltpu.CompilerParams(
            collective_id=0, has_side_effects=True, vmem_limit_bytes=56 * 1024 * 1024
        ),
    )(feats, weight, grad_out, neighbors, send_rows, send_counts.T)
    return pl.pallas_call(
        finish,
        out_shape=(
            jax.ShapeDtypeStruct((SHARE, VOX), BF16),
            jax.ShapeDtypeStruct((SHARE, VOX), F32),
            jax.ShapeDtypeStruct((KVOL, SHARE, C), F32),
        ),
        in_specs=[vmem] * 3,
        out_specs=[vmem] * 3,
        compiler_params=pltpu.CompilerParams(vmem_limit_bytes=60 * 1024 * 1024),
    )(codes, out_feats, grad_feats)


def solution(mesh):
    in_specs = (
        P("sub", "dom"),
        P(None, "sub", None),
        P("sub", "dom"),
        P(None, "dom"),
        P("dom", None),
        P(),
    )
    out_specs = (P("sub", "dom"), P("sub", "dom"), P(None, "sub", None))
    return jax.shard_map(body, mesh=mesh, in_specs=in_specs, out_specs=out_specs, check_vma=False)
```

```python
import math

import jax
import jax.numpy as jnp
from jax import lax
from jax.experimental import pallas as pl
from jax.experimental.pallas import tpu as pltpu
from jax.sharding import PartitionSpec as P

C = 256
KVOL = 27
CAP = 32
SUB = 4
NX = 4
NZ = 16
DOM = 2 * NX * NZ
SHARE = C // SUB
VOX = 384
HALO = 8 * CAP
COLS = VOX + HALO
GRID_Y = 8
DIRECTIONS = ((-1, -1), (-1, 0), (-1, 1), (0, -1), (0, 1), (1, -1), (1, 0), (1, 1))
HOPS = tuple(dx * GRID_Y + dy for dx, dy in DIRECTIONS)
CHUNKS = ((0, 15), (15, 27))
UNROLL = 3
STEPS = 128.0
TOP = 32000.0
MESH = pl.DeviceIdType.MESH
F32 = jnp.float32
BF16 = jnp.bfloat16
I16 = jnp.int16


def dot(a, b, dims):
    return lax.dot_general(a, b, (dims, ((), ())), preferred_element_type=F32)


NN = ((1,), (0,))
NT = ((1,), (1,))
TN = ((0,), (0,))


def encode(tiles, n):
    row = lax.broadcasted_iota(jnp.int32, tiles.shape, tiles.ndim - 2)
    tiles = jnp.where(row < n, tiles, 0.0)
    top = jnp.max(jnp.abs(tiles), axis=-2, keepdims=True)
    level = jnp.ceil(jnp.log2(jnp.maximum(top, 1e-33)) * STEPS)
    codes = jnp.round(tiles * (jnp.exp2(level * (-1.0 / STEPS)) * TOP))
    return jnp.where(row == n, level, codes).astype(jnp.int32).astype(I16)


def decode(codes, n):
    values = codes.astype(jnp.int32).astype(F32)
    level = values[..., n : n + 1, :]
    return values * (jnp.exp2(level * (1.0 / STEPS)) * (1.0 / TOP))


def kernel(
    feats_hbm, weight_hbm, grad_out_hbm, neighbors_hbm, send_rows_hbm, send_counts_hbm,
    out_feats_hbm, grad_feats_hbm, codes_hbm,
    feats, weight, grad_out, neighbors, send_rows, send_counts, out_feats, grad_feats, codes,
    nbr_t, onehot, picked, spread_hi, spread_lo, share_all, halo_out, halo_in, halo_all,
    table, wg, pair_in, x_out, x_in, x_sum, z_out, z_in, tg, tg_in, back_out, back_in,
    send, recv, local,
):
    me = lax.axis_index("dom")
    sub = lax.axis_index("sub")
    core = lax.rem(me, 2)
    z = lax.rem(me // 2, NZ)
    x = me // (2 * NZ)

    def wrap(i):
        return lax.rem(i + DOM, DOM)

    def at(xx, zz, cc):
        return (xx * NZ + zz) * 2 + cc

    twin = at(x, z, 1 - core)

    def x_peer(d):
        return lax.rem(x + d, NX)

    def z_peer(d):
        return lax.rem(z + d, NZ)

    def far_first(i):
        return NZ // 2 + ((i + 1) // 2) * (2 * lax.rem(i, 2) - 1)

    def y_peer(d):
        return lax.rem(sub + d, SUB)

    slots = {}

    def copy(name, index, src, dst, device):
        base = slots[name]
        return pltpu.make_async_remote_copy(
            src_ref=src, dst_ref=dst, send_sem=send.at[base + index], recv_sem=recv.at[base + index],
            device_id=device, device_id_type=MESH,
        )

    for base, name in enumerate(("share", "fwd", "tg")):
        slots[name] = 3 * base
    slots["halo"], slots["back"] = 9, 17
    slots["pair"], slots["gpair"] = 25, 27
    slots["x"], slots["gx"] = 29, 35
    slots["z"], slots["gz"] = 41, 73

    barrier = pltpu.get_barrier_semaphore()
    peers = [(me, y_peer(d)) for d in range(1, SUB)]
    peers += [(wrap(me + hop), sub) for hop in HOPS]
    peers += [(twin, sub)]
    peers += [(at(x_peer(d), z, core), sub) for d in range(1, NX)]
    def load(i):
        pairs = (
            (send_counts_hbm, send_counts), (send_rows_hbm, send_rows), (feats_hbm, feats),
            (neighbors_hbm, neighbors), (grad_out_hbm, grad_out), (weight_hbm, weight),
        )
        return pltpu.make_async_copy(pairs[i][0], pairs[i][1], local.at[i])

    def store(i):
        pairs = [(out_feats, out_feats_hbm), (grad_feats, grad_feats_hbm)]
        pairs += [(codes.at[c, half], codes_hbm.at[c, half]) for c in range(2) for half in (core, 1 - core)]
        return pltpu.make_async_copy(pairs[i][0], pairs[i][1], local.at[6 + i])

    with jax.named_scope("loads_first"):
        for i in range(3):
            load(i).start()

    with jax.named_scope("barrier_signals"):
        @pl.loop(0, NZ - 1)
        def _(i):
            peer = (at(x, z_peer(far_first(i)), core), sub)
            pl.semaphore_signal(barrier, inc=1, device_id=peer, device_id_type=MESH)

        for peer in peers:
            pl.semaphore_signal(barrier, inc=1, device_id=peer, device_id_type=MESH)

    with jax.named_scope("loads"):
        for i in range(3, 6):
            load(i).start()

    with jax.named_scope("boundary_tiles"):
        for i in range(3):
            load(i).wait()
        lane = lax.broadcasted_iota(jnp.int32, (1, HALO), 1)
        mine = send_counts[...]
        mine = jnp.where(lax.broadcasted_iota(jnp.int32, (8, DOM), 1) == me, mine, 0).astype(F32)
        mine = jnp.sum(mine, axis=1, keepdims=True).astype(jnp.int32)
        count = jnp.zeros((1, HALO), jnp.int32)
        for n in range(8):
            count = jnp.where(lane // CAP == n, mine[n : n + 1, :], count)
        rows = jnp.where(lane % CAP < count, send_rows[...], -1)
        pick = (lax.broadcasted_iota(jnp.int32, (VOX, HALO), 0) == rows).astype(F32).astype(BF16)
        outgoing = dot(feats[...], pick, NN).T.reshape(8, 2, 16, SHARE)
        halo_out[...] = jnp.concatenate([outgoing[:, 0], outgoing[:, 1]], axis=-1).astype(BF16)

    with jax.named_scope("barrier_wait"):
        pl.semaphore_wait(barrier, len(peers) + NZ - 1)

    def share_copy(d):
        return copy("share", d - 1, feats, share_all.at[sub], (me, y_peer(d)))

    def halo_copy(n):
        return copy("halo", n, halo_out.at[n], halo_in.at[n], (wrap(me + HOPS[n]), sub))

    def fwd_copy(d):
        return copy("fwd", d - 1, halo_in, halo_all.at[sub], (me, y_peer(d)))

    with jax.named_scope("first_sends"):
        for n in range(8):
            halo_copy(n).start()
        for d in range(1, SUB):
            share_copy(d).start()
        share_all[sub] = feats[...]

    with jax.named_scope("transpose_maps"):
        for i in (3, 4, 5):
            load(i).wait()
        nbr_t[...] = jnp.concatenate(
            [neighbors[...], jnp.zeros((128 - KVOL, VOX), jnp.int32)], axis=0
        ).T
        col = lax.broadcasted_iota(jnp.int32, (1, COLS), 1)
        r = col - VOX
        slot = jnp.where(col < VOX, col, VOX + ((r % 128) // 16) * CAP + (r // 128) * 16 + r % 16)

    with jax.named_scope("onehot"):
        @pl.loop(0, KVOL // UNROLL)
        def _(g):
            now = nbr_t[...]
            nbr_t[...] = pltpu.roll(now, 128 - UNROLL, 1)
            for j in range(UNROLL):
                onehot[g * UNROLL + j] = (now[:, j : j + 1] == slot).astype(F32).astype(BF16)

    def spread(first, last):
        @pl.loop(first, last)
        def _(g):
            for j in range(UNROLL):
                k = g * UNROLL + j
                total = dot(grad_out[...], onehot[k], NN)
                high = total.astype(BF16)
                spread_hi[k] = high
                spread_lo[k] = (total - high.astype(F32)).astype(BF16)

    with jax.named_scope("spread_a"):
        spread(0, 5)

    def gather_own(first, last):
        @pl.loop(first // UNROLL, last // UNROLL)
        def _(g):
            hot = onehot[pl.ds(g * UNROLL, UNROLL), :, 0:VOX].reshape(UNROLL * VOX, VOX)
            got = dot(hot, table[0:VOX], NN).astype(BF16)
            picked[pl.ds(g * UNROLL, UNROLL)] = got.reshape(UNROLL, VOX, C)

    with jax.named_scope("table_own"):
        for d in range(1, SUB):
            share_copy(d).wait_recv()
        table[0:VOX] = share_all[...].reshape(C, VOX).T
    with jax.named_scope("gather_own_a"):
        gather_own(0, 9)

    with jax.named_scope("halo_arrival"):
        for n in range(8):
            halo_copy(n).wait_recv()
        for d in range(1, SUB):
            fwd_copy(d).start()
        halo_all[sub] = halo_in[...]

    with jax.named_scope("gather_own_b"):
        gather_own(9, 27)

    with jax.named_scope("table_halo"):
        for d in range(1, SUB):
            fwd_copy(d).wait_recv()
        tiles = halo_all[...].reshape(SUB, 128, 128)
        for half in range(2):
            lanes = slice(half * SHARE, (half + 1) * SHARE)
            table[VOX + half * 128 : VOX + (half + 1) * 128] = jnp.concatenate(
                [tiles[s][:, lanes] for s in range(SUB)], axis=1
            )

    def pair_copy(c):
        return copy("pair", c, wg.at[c, 1 - core], pair_in.at[c], (twin, sub))

    def x_copy(c, d):
        return copy("x", 3 * c + d - 1, x_out.at[c, d - 1], x_in.at[c, d - 1], (at(x_peer(d), z, core), sub))

    def own_tile(zz):
        return pl.ds(pl.multiple_of(zz * 16, 16), 16)

    def z_copy(c, d):
        return copy("z", 16 * c + d - 1, z_out.at[c, own_tile(z_peer(d))], z_in.at[c, d - 1], (at(x, z_peer(d), core), sub))

    def gz_copy(c, d):
        ref = codes.at[c, core, x, own_tile(z)]
        return copy("gz", 16 * c + d - 1, ref, ref, (at(x, z_peer(d), core), sub))

    def gz_arrival(c, d):
        ref = codes.at[c, core, x, own_tile(z_peer(NZ - d))]
        return copy("gz", 16 * c + d - 1, ref, ref, (at(x, z_peer(d), core), sub))

    def gx_copy(c, d):
        ref = codes.at[c, core, x]
        return copy("gx", 3 * c + d - 1, ref, ref, (at(x_peer(d), z, core), sub))

    def gx_arrival(c, d):
        ref = codes.at[c, core, x_peer(NX - d)]
        return copy("gx", 3 * c + d - 1, ref, ref, (at(x_peer(d), z, core), sub))

    def gpair_copy(c):
        ref = codes.at[c, core]
        return copy("gpair", c, ref, ref, (twin, sub))

    def gpair_arrival(c):
        ref = codes.at[c, 1 - core]
        return copy("gpair", c, ref, ref, (twin, sub))

    def gather(c, first, last):
        lo = CHUNKS[c][0]

        @pl.loop(first // UNROLL, last // UNROLL)
        def _(g):
            k0 = g * UNROLL
            hot = onehot[pl.ds(k0, UNROLL), :, VOX:COLS].reshape(UNROLL * VOX, HALO)
            got = dot(hot, table[VOX:COLS], NN).astype(BF16).reshape(UNROLL, VOX, C)
            got = got + picked[pl.ds(k0, UNROLL)]
            picked[pl.ds(k0, UNROLL)] = got
            for j in range(UNROLL):
                fresh = dot(grad_out[...], got[j], NN)
                for cc in range(2):
                    for xx in range(NX):
                        r0, l0 = cc * 32 + (xx // 2) * 16, (xx % 2) * 128
                        wg[c, cc, xx, pl.ds(k0 + j - lo, 16, stride=16), :] = fresh[r0 : r0 + 16, l0 : l0 + 128]

    def pair_to_x(c):
        lo, hi = CHUNKS[c]
        pair_copy(c).wait_recv()
        for d in (2, 1, 3):
            both = wg[c, core, x_peer(d)] + pair_in[c, x_peer(d)]
            x_out[c, d - 1] = encode(both.reshape(16, 16, 128), hi - lo).reshape(256, 128)
            x_copy(c, d).start()

    def x_to_z(c):
        lo, hi = CHUNKS[c]
        for d in range(1, NX):
            x_copy(c, d).wait_recv()
        total = (wg[c, core, x] + pair_in[c, x]).reshape(16, 16, 128)
        for d in range(1, NX):
            total = total + decode(x_in[c, d - 1].reshape(16, 16, 128), hi - lo)
        x_sum[c] = total.reshape(256, 128)
        z_out[c] = encode(total, hi - lo).reshape(256, 128)

        @pl.loop(0, NZ - 1)
        def _(i):
            z_copy(c, far_first(i)).start()

    with jax.named_scope("wg_rows"):
        for c, (lo, hi) in enumerate(CHUNKS):
            for row in range(hi - lo, 16):
                for cc in range(2):
                    for xx in range(NX):
                        wg[c, cc, xx, pl.ds(row, 16, stride=16), :] = jnp.zeros((16, 128), F32)

    with jax.named_scope("gather_a"):
        gather(0, 0, 15)
    with jax.named_scope("pair_a"):
        pair_copy(0).start()
    with jax.named_scope("gather_b"):
        gather(1, 15, 21)
    with jax.named_scope("pair_to_x_a"):
        pair_to_x(0)
    with jax.named_scope("gather_c"):
        gather(1, 21, 27)
    with jax.named_scope("pair_b"):
        pair_copy(1).start()

    with jax.named_scope("pair_to_x_b"):
        pair_to_x(1)
    with jax.named_scope("spread_b"):
        spread(5, 9)

    with jax.named_scope("x_to_z_a"):
        x_to_z(0)

    with jax.named_scope("table_grad"):
        total = None
        for k in range(0, KVOL, 4):
            n = min(4, KVOL - k)
            w = weight[k : k + n].reshape(n * SHARE, C)
            for part in (spread_hi, spread_lo):
                term = dot(w, part[k : k + n].reshape(n * SHARE, COLS), TN)
                total = term if total is None else total + term
        tg[...] = total.reshape(SUB, SHARE, COLS)

    def tg_copy(d):
        return copy("tg", d - 1, tg.at[y_peer(d)], tg_in.at[d - 1], (me, y_peer(d)))

    with jax.named_scope("tg_sends"):
        for d in range(1, SUB):
            tg_copy(d).start()

    with jax.named_scope("x_to_z_b"):
        x_to_z(1)

    def z_reduce(c):
        lo, hi = CHUNKS[c]

        @pl.loop(1, NZ)
        def _(d):
            z_copy(c, d).wait_recv()

        total = x_sum[c, own_tile(z)] + jnp.sum(decode(z_in[c], hi - lo), axis=0)
        scaled = total * (1.0 / math.sqrt(VOX * DOM))
        codes[c, core, x, own_tile(z)] = encode(scaled, hi - lo)

        @pl.loop(0, NZ - 1)
        def _(i):
            gz_copy(c, far_first(i)).start()

    def z_to_x(c):
        @pl.loop(1, NZ)
        def _(d):
            gz_arrival(c, d).wait_recv()

        for d in (2, 1, 3):
            gx_copy(c, d).start()

    def x_to_pair(c):
        for d in range(1, NX):
            gx_arrival(c, d).wait_recv()
        gpair_copy(c).start()
        store(2 + 2 * c).start()

    with jax.named_scope("z_reduce_a"):
        z_reduce(0)

    with jax.named_scope("tg_sum"):
        for d in range(1, SUB):
            tg_copy(d).wait_recv()
        mine_tg = tg[sub] + tg_in[0] + tg_in[1] + tg_in[2]
        tail = mine_tg[:, VOX:].T
        back_out[...] = jnp.concatenate([tail[:128], tail[128:]], axis=1).reshape(8, 16, 128)

    def back_copy(n):
        return copy("back", n, back_out.at[n], back_in.at[n], (wrap(me - HOPS[n]), sub))

    with jax.named_scope("back_sends"):
        for n in range(8):
            back_copy(n).start()

    with jax.named_scope("out_feats"):
        def out_step(g, acc):
            for j in range(UNROLL):
                acc = acc + dot(weight[g * UNROLL + j], picked[g * UNROLL + j], NT)
            return acc

        out_feats[...] = lax.fori_loop(0, KVOL // UNROLL, out_step, jnp.zeros((SHARE, VOX), F32)).astype(BF16)
        store(0).start()

    with jax.named_scope("z_reduce_b"):
        z_reduce(1)

    with jax.named_scope("z_back"):
        z_to_x(0)
        z_to_x(1)
    with jax.named_scope("drain_early"):
        for d in range(1, SUB):
            share_copy(d).wait_send()
            fwd_copy(d).wait_send()
            tg_copy(d).wait_send()
        for n in range(8):
            halo_copy(n).wait_send()
            back_copy(n).wait_send()
        for c in range(2):
            pair_copy(c).wait_send()
            for d in range(1, NX):
                x_copy(c, d).wait_send()

            @pl.loop(1, NZ)
            def _(d):
                z_copy(c, d).wait_send()
                gz_copy(c, d).wait_send()

    with jax.named_scope("x_back"):
        x_to_pair(0)
        x_to_pair(1)

    with jax.named_scope("grad_feats"):
        for n in range(8):
            back_copy(n).wait_recv()
        back = back_in[...]
        back = jnp.concatenate([back[:, :, :SHARE][:, None], back[:, :, SHARE:][:, None]], axis=1)
        back = back.reshape(HALO, SHARE).T
        back_hi = back.astype(BF16)
        back_lo = (back - back_hi.astype(F32)).astype(BF16)
        grad_feats[...] = mine_tg[:, :VOX] + dot(back_hi, pick, NT) + dot(back_lo, pick, NT)
        store(1).start()

    with jax.named_scope("pair_back"):
        for c in range(2):
            gpair_arrival(c).wait_recv()
            store(3 + 2 * c).start()

    with jax.named_scope("drain"):
        for c in range(2):
            gpair_copy(c).wait_send()
            for d in range(1, NX):
                gx_copy(c, d).wait_send()
    with jax.named_scope("stores"):
        for i in range(6):
            store(i).wait()


def finish(codes, out_in, feats_in, out_feats, grad_feats, grad_weight):
    out_feats[...] = out_in[...]
    grad_feats[...] = feats_in[...]
    for c, (lo, hi) in enumerate(CHUNKS):
        for cc in range(2):
            for xx in range(NX):
                values = decode(codes[c, cc, xx].reshape(16, 16, 128), hi - lo)
                r0, l0 = cc * 32 + (xx // 2) * 16, (xx % 2) * 128
                values = jnp.swapaxes(values, 0, 1)
                grad_weight[lo:hi, r0 : r0 + 16, l0 : l0 + 128] = values[: hi - lo]


def body(feats, weight, grad_out, neighbors, send_rows, send_counts):
    hbm = pl.BlockSpec(memory_space=pltpu.HBM)
    vmem = pl.BlockSpec(memory_space=pltpu.VMEM)
    out_feats, grad_feats, codes = pl.pallas_call(
        kernel,
        out_shape=(
            jax.ShapeDtypeStruct((SHARE, VOX), BF16),
            jax.ShapeDtypeStruct((SHARE, VOX), F32),
            jax.ShapeDtypeStruct((2, 2, NX, 256, 128), I16),
        ),
        in_specs=[hbm] * 6,
        out_specs=[hbm] * 3,
        scratch_shapes=[
            pltpu.VMEM((SHARE, VOX), BF16),
            pltpu.VMEM((KVOL, SHARE, C), BF16),
            pltpu.VMEM((SHARE, VOX), BF16),
            pltpu.VMEM((KVOL, VOX), jnp.int32),
            pltpu.VMEM((1, HALO), jnp.int32),
            pltpu.VMEM((8, DOM), jnp.int32),
            pltpu.VMEM((SHARE, VOX), BF16),
            pltpu.VMEM((SHARE, VOX), F32),
            pltpu.VMEM((2, 2, NX, 256, 128), I16),
            pltpu.VMEM((VOX, 128), jnp.int32),
            pltpu.VMEM((KVOL, VOX, COLS), BF16),
            pltpu.VMEM((KVOL, VOX, C), BF16),
            pltpu.VMEM((KVOL + 1, SHARE, COLS), BF16),
            pltpu.VMEM((KVOL + 1, SHARE, COLS), BF16),
            pltpu.VMEM((SUB, SHARE, VOX), BF16),
            pltpu.VMEM((8, 16, 128), BF16),
            pltpu.VMEM((8, 16, 128), BF16),
            pltpu.VMEM((SUB, 8, 16, 128), BF16),
            pltpu.VMEM((COLS, C), BF16),
            pltpu.VMEM((2, 2, NX, 256, 128), F32),
            pltpu.VMEM((2, NX, 256, 128), F32),
            pltpu.VMEM((2, NX - 1, 256, 128), I16),
            pltpu.VMEM((2, NX - 1, 256, 128), I16),
            pltpu.VMEM((2, 256, 128), F32),
            pltpu.VMEM((2, 256, 128), I16),
            pltpu.VMEM((2, NZ - 1, 16, 128), I16),
            pltpu.VMEM((SUB, SHARE, COLS), F32),
            pltpu.VMEM((SUB - 1, SHARE, COLS), F32),
            pltpu.VMEM((8, 16, 128), F32),
            pltpu.VMEM((8, 16, 128), F32),
            pltpu.SemaphoreType.DMA((105,)),
            pltpu.SemaphoreType.DMA((105,)),
            pltpu.SemaphoreType.DMA((12,)),
        ],
        compiler_params=pltpu.CompilerParams(
            collective_id=0, has_side_effects=True, vmem_limit_bytes=56 * 1024 * 1024
        ),
    )(feats, weight, grad_out, neighbors, send_rows, send_counts.T)
    return pl.pallas_call(
        finish,
        out_shape=(
            jax.ShapeDtypeStruct((SHARE, VOX), BF16),
            jax.ShapeDtypeStruct((SHARE, VOX), F32),
            jax.ShapeDtypeStruct((KVOL, SHARE, C), F32),
        ),
        in_specs=[vmem] * 3,
        out_specs=[vmem] * 3,
        compiler_params=pltpu.CompilerParams(vmem_limit_bytes=60 * 1024 * 1024),
    )(codes, out_feats, grad_feats)


def solution(mesh):
    in_specs = (
        P("sub", "dom"),
        P(None, "sub", None),
        P("sub", "dom"),
        P(None, "dom"),
        P("dom", None),
        P(),
    )
    out_specs = (P("sub", "dom"), P("sub", "dom"), P(None, "sub", None))
    return jax.shard_map(body, mesh=mesh, in_specs=in_specs, out_specs=out_specs, check_vma=False)
```

```python
import math

import jax
import jax.numpy as jnp
from jax import lax
from jax.experimental import pallas as pl
from jax.experimental.pallas import tpu as pltpu
from jax.sharding import PartitionSpec as P

C = 256
KVOL = 27
CAP = 32
SUB = 4
NX = 4
NZ = 16
DOM = 2 * NX * NZ
SHARE = C // SUB
VOX = 384
HALO = 8 * CAP
COLS = VOX + HALO
GRID_Y = 8
DIRECTIONS = ((-1, -1), (-1, 0), (-1, 1), (0, -1), (0, 1), (1, -1), (1, 0), (1, 1))
HOPS = tuple(dx * GRID_Y + dy for dx, dy in DIRECTIONS)
CHUNKS = ((0, 15), (15, 27))
UNROLL = 3
STEPS = 128.0
TOP = 32000.0
MESH = pl.DeviceIdType.MESH
F32 = jnp.float32
BF16 = jnp.bfloat16
I16 = jnp.int16


def dot(a, b, dims):
    return lax.dot_general(a, b, (dims, ((), ())), preferred_element_type=F32)


NN = ((1,), (0,))
NT = ((1,), (1,))
TN = ((0,), (0,))


def encode(tiles, n):
    row = lax.broadcasted_iota(jnp.int32, tiles.shape, tiles.ndim - 2)
    tiles = jnp.where(row < n, tiles, 0.0)
    top = jnp.max(jnp.abs(tiles), axis=-2, keepdims=True)
    level = jnp.ceil(jnp.log2(jnp.maximum(top, 1e-33)) * STEPS)
    codes = jnp.round(tiles * (jnp.exp2(level * (-1.0 / STEPS)) * TOP))
    return jnp.where(row == n, level, codes).astype(jnp.int32).astype(I16)


def decode(codes, n):
    values = codes.astype(jnp.int32).astype(F32)
    level = values[..., n : n + 1, :]
    return values * (jnp.exp2(level * (1.0 / STEPS)) * (1.0 / TOP))


def kernel(
    feats_hbm, weight_hbm, grad_out_hbm, neighbors_hbm, send_rows_hbm, send_counts_hbm,
    out_feats, grad_feats, codes,
    feats, weight, grad_out, neighbors, send_rows, send_counts,
    nbr_t, onehot, picked, spread_hi, spread_lo, share_all, halo_out, halo_in, halo_all,
    table, wg, pair_in, x_out, x_in, x_sum, z_out, z_in, tg, tg_in, back_out, back_in,
    send, recv, local,
):
    me = lax.axis_index("dom")
    sub = lax.axis_index("sub")
    core = lax.rem(me, 2)
    z = lax.rem(me // 2, NZ)
    x = me // (2 * NZ)

    def wrap(i):
        return lax.rem(i + DOM, DOM)

    def at(xx, zz, cc):
        return (xx * NZ + zz) * 2 + cc

    twin = at(x, z, 1 - core)

    def x_peer(d):
        return lax.rem(x + d, NX)

    def z_peer(d):
        return lax.rem(z + d, NZ)

    def far_first(i):
        return NZ // 2 + ((i + 1) // 2) * (2 * lax.rem(i, 2) - 1)

    def y_peer(d):
        return lax.rem(sub + d, SUB)

    slots = {}

    def copy(name, index, src, dst, device):
        base = slots[name]
        return pltpu.make_async_remote_copy(
            src_ref=src, dst_ref=dst, send_sem=send.at[base + index], recv_sem=recv.at[base + index],
            device_id=device, device_id_type=MESH,
        )

    for base, name in enumerate(("share", "fwd", "tg")):
        slots[name] = 3 * base
    slots["halo"], slots["back"] = 9, 17
    slots["pair"], slots["gpair"] = 25, 27
    slots["x"], slots["gx"] = 29, 35
    slots["z"], slots["gz"] = 41, 73

    barrier = pltpu.get_barrier_semaphore()
    peers = [(me, y_peer(d)) for d in range(1, SUB)]
    peers += [(wrap(me + hop), sub) for hop in HOPS]
    peers += [(twin, sub)]
    peers += [(at(x_peer(d), z, core), sub) for d in range(1, NX)]
    def load(i):
        pairs = (
            (send_counts_hbm, send_counts), (send_rows_hbm, send_rows), (feats_hbm, feats),
            (neighbors_hbm, neighbors), (grad_out_hbm, grad_out), (weight_hbm, weight),
        )
        return pltpu.make_async_copy(pairs[i][0], pairs[i][1], local.at[i])

    with jax.named_scope("loads_first"):
        for i in range(3):
            load(i).start()

    with jax.named_scope("barrier_signals"):
        @pl.loop(0, NZ - 1)
        def _(i):
            peer = (at(x, z_peer(far_first(i)), core), sub)
            pl.semaphore_signal(barrier, inc=1, device_id=peer, device_id_type=MESH)

        for peer in peers:
            pl.semaphore_signal(barrier, inc=1, device_id=peer, device_id_type=MESH)

    with jax.named_scope("loads"):
        for i in range(3, 6):
            load(i).start()

    with jax.named_scope("boundary_tiles"):
        for i in range(3):
            load(i).wait()
        lane = lax.broadcasted_iota(jnp.int32, (1, HALO), 1)
        mine = send_counts[...]
        mine = jnp.where(lax.broadcasted_iota(jnp.int32, (8, DOM), 1) == me, mine, 0).astype(F32)
        mine = jnp.sum(mine, axis=1, keepdims=True).astype(jnp.int32)
        count = jnp.zeros((1, HALO), jnp.int32)
        for n in range(8):
            count = jnp.where(lane // CAP == n, mine[n : n + 1, :], count)
        rows = jnp.where(lane % CAP < count, send_rows[...], -1)
        pick = (lax.broadcasted_iota(jnp.int32, (VOX, HALO), 0) == rows).astype(F32).astype(BF16)
        outgoing = dot(feats[...], pick, NN).T.reshape(8, 2, 16, SHARE)
        halo_out[...] = jnp.concatenate([outgoing[:, 0], outgoing[:, 1]], axis=-1).astype(BF16)

    with jax.named_scope("barrier_wait"):
        pl.semaphore_wait(barrier, len(peers) + NZ - 1)

    def share_copy(d):
        return copy("share", d - 1, feats, share_all.at[sub], (me, y_peer(d)))

    def halo_copy(n):
        return copy("halo", n, halo_out.at[n], halo_in.at[n], (wrap(me + HOPS[n]), sub))

    def fwd_copy(d):
        return copy("fwd", d - 1, halo_in, halo_all.at[sub], (me, y_peer(d)))

    with jax.named_scope("first_sends"):
        for n in range(8):
            halo_copy(n).start()
        for d in range(1, SUB):
            share_copy(d).start()
        share_all[sub] = feats[...]

    with jax.named_scope("transpose_maps"):
        for i in (3, 4, 5):
            load(i).wait()
        nbr_t[...] = jnp.concatenate(
            [neighbors[...], jnp.zeros((128 - KVOL, VOX), jnp.int32)], axis=0
        ).T
        col = lax.broadcasted_iota(jnp.int32, (1, COLS), 1)
        r = col - VOX
        slot = jnp.where(col < VOX, col, VOX + ((r % 128) // 16) * CAP + (r // 128) * 16 + r % 16)

    with jax.named_scope("onehot"):
        @pl.loop(0, KVOL // UNROLL)
        def _(g):
            now = nbr_t[...]
            nbr_t[...] = pltpu.roll(now, 128 - UNROLL, 1)
            for j in range(UNROLL):
                onehot[g * UNROLL + j] = (now[:, j : j + 1] == slot).astype(F32).astype(BF16)

    def spread(first, last):
        @pl.loop(first, last)
        def _(g):
            for j in range(UNROLL):
                k = g * UNROLL + j
                total = dot(grad_out[...], onehot[k], NN)
                high = total.astype(BF16)
                spread_hi[k] = high
                spread_lo[k] = (total - high.astype(F32)).astype(BF16)

    with jax.named_scope("spread_a"):
        spread(0, 5)

    def gather_own(first, last):
        @pl.loop(first // UNROLL, last // UNROLL)
        def _(g):
            hot = onehot[pl.ds(g * UNROLL, UNROLL), :, 0:VOX].reshape(UNROLL * VOX, VOX)
            got = dot(hot, table[0:VOX], NN).astype(BF16)
            picked[pl.ds(g * UNROLL, UNROLL)] = got.reshape(UNROLL, VOX, C)

    with jax.named_scope("table_own"):
        for d in range(1, SUB):
            share_copy(d).wait_recv()
        table[0:VOX] = share_all[...].reshape(C, VOX).T
    with jax.named_scope("gather_own_a"):
        gather_own(0, 9)

    with jax.named_scope("halo_arrival"):
        for n in range(8):
            halo_copy(n).wait_recv()
        for d in range(1, SUB):
            fwd_copy(d).start()
        halo_all[sub] = halo_in[...]

    with jax.named_scope("gather_own_b"):
        gather_own(9, 27)

    with jax.named_scope("table_halo"):
        for d in range(1, SUB):
            fwd_copy(d).wait_recv()
        tiles = halo_all[...].reshape(SUB, 128, 128)
        for half in range(2):
            lanes = slice(half * SHARE, (half + 1) * SHARE)
            table[VOX + half * 128 : VOX + (half + 1) * 128] = jnp.concatenate(
                [tiles[s][:, lanes] for s in range(SUB)], axis=1
            )

    def pair_copy(c):
        return copy("pair", c, wg.at[c, 1 - core], pair_in.at[c], (twin, sub))

    def x_copy(c, d):
        return copy("x", 3 * c + d - 1, x_out.at[c, d - 1], x_in.at[c, d - 1], (at(x_peer(d), z, core), sub))

    def own_tile(zz):
        return pl.ds(pl.multiple_of(zz * 16, 16), 16)

    def z_copy(c, d):
        return copy("z", 16 * c + d - 1, z_out.at[c, own_tile(z_peer(d))], z_in.at[c, d - 1], (at(x, z_peer(d), core), sub))

    def gz_copy(c, d):
        ref = codes.at[c, core, x, own_tile(z)]
        return copy("gz", 16 * c + d - 1, ref, ref, (at(x, z_peer(d), core), sub))

    def gz_arrival(c, d):
        ref = codes.at[c, core, x, own_tile(z_peer(NZ - d))]
        return copy("gz", 16 * c + d - 1, ref, ref, (at(x, z_peer(d), core), sub))

    def gx_copy(c, d):
        ref = codes.at[c, core, x]
        return copy("gx", 3 * c + d - 1, ref, ref, (at(x_peer(d), z, core), sub))

    def gx_arrival(c, d):
        ref = codes.at[c, core, x_peer(NX - d)]
        return copy("gx", 3 * c + d - 1, ref, ref, (at(x_peer(d), z, core), sub))

    def gpair_copy(c):
        ref = codes.at[c, core]
        return copy("gpair", c, ref, ref, (twin, sub))

    def gpair_arrival(c):
        ref = codes.at[c, 1 - core]
        return copy("gpair", c, ref, ref, (twin, sub))

    def gather(c, first, last):
        lo = CHUNKS[c][0]

        @pl.loop(first // UNROLL, last // UNROLL)
        def _(g):
            k0 = g * UNROLL
            hot = onehot[pl.ds(k0, UNROLL), :, VOX:COLS].reshape(UNROLL * VOX, HALO)
            got = dot(hot, table[VOX:COLS], NN).astype(BF16).reshape(UNROLL, VOX, C)
            got = got + picked[pl.ds(k0, UNROLL)]
            picked[pl.ds(k0, UNROLL)] = got
            for j in range(UNROLL):
                fresh = dot(grad_out[...], got[j], NN)
                for cc in range(2):
                    for xx in range(NX):
                        r0, l0 = cc * 32 + (xx // 2) * 16, (xx % 2) * 128
                        wg[c, cc, xx, pl.ds(k0 + j - lo, 16, stride=16), :] = fresh[r0 : r0 + 16, l0 : l0 + 128]

    def pair_to_x(c):
        lo, hi = CHUNKS[c]
        pair_copy(c).wait_recv()
        for d in (2, 1, 3):
            both = wg[c, core, x_peer(d)] + pair_in[c, x_peer(d)]
            x_out[c, d - 1] = encode(both.reshape(16, 16, 128), hi - lo).reshape(256, 128)
            x_copy(c, d).start()

    def x_to_z(c):
        lo, hi = CHUNKS[c]
        for d in range(1, NX):
            x_copy(c, d).wait_recv()
        total = (wg[c, core, x] + pair_in[c, x]).reshape(16, 16, 128)
        for d in range(1, NX):
            total = total + decode(x_in[c, d - 1].reshape(16, 16, 128), hi - lo)
        x_sum[c] = total.reshape(256, 128)
        z_out[c] = encode(total, hi - lo).reshape(256, 128)

        @pl.loop(0, NZ - 1)
        def _(i):
            z_copy(c, far_first(i)).start()

    with jax.named_scope("wg_rows"):
        for c, (lo, hi) in enumerate(CHUNKS):
            for row in range(hi - lo, 16):
                for cc in range(2):
                    for xx in range(NX):
                        wg[c, cc, xx, pl.ds(row, 16, stride=16), :] = jnp.zeros((16, 128), F32)

    with jax.named_scope("gather_a"):
        gather(0, 0, 15)
    with jax.named_scope("pair_a"):
        pair_copy(0).start()
    with jax.named_scope("gather_b"):
        gather(1, 15, 21)
    with jax.named_scope("pair_to_x_a"):
        pair_to_x(0)
    with jax.named_scope("gather_c"):
        gather(1, 21, 27)
    with jax.named_scope("pair_b"):
        pair_copy(1).start()

    with jax.named_scope("pair_to_x_b"):
        pair_to_x(1)
    with jax.named_scope("spread_b"):
        spread(5, 9)

    with jax.named_scope("x_to_z_a"):
        x_to_z(0)

    with jax.named_scope("table_grad"):
        total = None
        for k in range(0, KVOL, 4):
            n = min(4, KVOL - k)
            w = weight[k : k + n].reshape(n * SHARE, C)
            for part in (spread_hi, spread_lo):
                term = dot(w, part[k : k + n].reshape(n * SHARE, COLS), TN)
                total = term if total is None else total + term
        tg[...] = total.reshape(SUB, SHARE, COLS)

    def tg_copy(d):
        return copy("tg", d - 1, tg.at[y_peer(d)], tg_in.at[d - 1], (me, y_peer(d)))

    with jax.named_scope("tg_sends"):
        for d in range(1, SUB):
            tg_copy(d).start()

    with jax.named_scope("x_to_z_b"):
        x_to_z(1)

    def z_reduce(c):
        lo, hi = CHUNKS[c]

        @pl.loop(1, NZ)
        def _(d):
            z_copy(c, d).wait_recv()

        total = x_sum[c, own_tile(z)] + jnp.sum(decode(z_in[c], hi - lo), axis=0)
        scaled = total * (1.0 / math.sqrt(VOX * DOM))
        codes[c, core, x, own_tile(z)] = encode(scaled, hi - lo)

        @pl.loop(0, NZ - 1)
        def _(i):
            gz_copy(c, far_first(i)).start()

    def z_to_x(c):
        @pl.loop(1, NZ)
        def _(d):
            gz_arrival(c, d).wait_recv()

        for d in (2, 1, 3):
            gx_copy(c, d).start()

    def x_to_pair(c):
        for d in range(1, NX):
            gx_arrival(c, d).wait_recv()
        gpair_copy(c).start()

    with jax.named_scope("z_reduce_a"):
        z_reduce(0)

    with jax.named_scope("tg_sum"):
        for d in range(1, SUB):
            tg_copy(d).wait_recv()
        mine_tg = tg[sub] + tg_in[0] + tg_in[1] + tg_in[2]
        tail = mine_tg[:, VOX:].T
        back_out[...] = jnp.concatenate([tail[:128], tail[128:]], axis=1).reshape(8, 16, 128)

    def back_copy(n):
        return copy("back", n, back_out.at[n], back_in.at[n], (wrap(me - HOPS[n]), sub))

    with jax.named_scope("back_sends"):
        for n in range(8):
            back_copy(n).start()

    with jax.named_scope("out_feats"):
        def out_step(g, acc):
            for j in range(UNROLL):
                acc = acc + dot(weight[g * UNROLL + j], picked[g * UNROLL + j], NT)
            return acc

        out_feats[...] = lax.fori_loop(0, KVOL // UNROLL, out_step, jnp.zeros((SHARE, VOX), F32)).astype(BF16)

    with jax.named_scope("z_reduce_b"):
        z_reduce(1)

    with jax.named_scope("z_back"):
        z_to_x(0)
        z_to_x(1)
    with jax.named_scope("drain_early"):
        for d in range(1, SUB):
            share_copy(d).wait_send()
            fwd_copy(d).wait_send()
            tg_copy(d).wait_send()
        for n in range(8):
            halo_copy(n).wait_send()
            back_copy(n).wait_send()
        for c in range(2):
            pair_copy(c).wait_send()
            for d in range(1, NX):
                x_copy(c, d).wait_send()

            @pl.loop(1, NZ)
            def _(d):
                z_copy(c, d).wait_send()
                gz_copy(c, d).wait_send()

    with jax.named_scope("x_back"):
        x_to_pair(0)
        x_to_pair(1)

    with jax.named_scope("grad_feats"):
        for n in range(8):
            back_copy(n).wait_recv()
        back = back_in[...]
        back = jnp.concatenate([back[:, :, :SHARE][:, None], back[:, :, SHARE:][:, None]], axis=1)
        back = back.reshape(HALO, SHARE).T
        back_hi = back.astype(BF16)
        back_lo = (back - back_hi.astype(F32)).astype(BF16)
        grad_feats[...] = mine_tg[:, :VOX] + dot(back_hi, pick, NT) + dot(back_lo, pick, NT)

    with jax.named_scope("pair_back"):
        for c in range(2):
            gpair_arrival(c).wait_recv()

    with jax.named_scope("drain"):
        for c in range(2):
            gpair_copy(c).wait_send()
            for d in range(1, NX):
                gx_copy(c, d).wait_send()


def finish(codes, out_in, feats_in, out_feats, grad_feats, grad_weight):
    out_feats[...] = out_in[...]
    grad_feats[...] = feats_in[...]
    for c, (lo, hi) in enumerate(CHUNKS):
        for cc in range(2):
            for xx in range(NX):
                values = decode(codes[c, cc, xx].reshape(16, 16, 128), hi - lo)
                r0, l0 = cc * 32 + (xx // 2) * 16, (xx % 2) * 128
                values = jnp.swapaxes(values, 0, 1)
                grad_weight[lo:hi, r0 : r0 + 16, l0 : l0 + 128] = values[: hi - lo]


def body(feats, weight, grad_out, neighbors, send_rows, send_counts):
    hbm = pl.BlockSpec(memory_space=pltpu.HBM)
    vmem = pl.BlockSpec(memory_space=pltpu.VMEM)
    out_feats, grad_feats, codes = pl.pallas_call(
        kernel,
        out_shape=(
            pltpu.VMEM((SHARE, VOX), BF16),
            pltpu.VMEM((SHARE, VOX), F32),
            pltpu.VMEM((2, 2, NX, 256, 128), I16),
        ),
        in_specs=[hbm] * 6,
        out_specs=[vmem] * 3,
        scratch_shapes=[
            pltpu.VMEM((SHARE, VOX), BF16),
            pltpu.VMEM((KVOL, SHARE, C), BF16),
            pltpu.VMEM((SHARE, VOX), BF16),
            pltpu.VMEM((KVOL, VOX), jnp.int32),
            pltpu.VMEM((1, HALO), jnp.int32),
            pltpu.VMEM((8, DOM), jnp.int32),
            pltpu.VMEM((VOX, 128), jnp.int32),
            pltpu.VMEM((KVOL, VOX, COLS), BF16),
            pltpu.VMEM((KVOL, VOX, C), BF16),
            pltpu.VMEM((KVOL + 1, SHARE, COLS), BF16),
            pltpu.VMEM((KVOL + 1, SHARE, COLS), BF16),
            pltpu.VMEM((SUB, SHARE, VOX), BF16),
            pltpu.VMEM((8, 16, 128), BF16),
            pltpu.VMEM((8, 16, 128), BF16),
            pltpu.VMEM((SUB, 8, 16, 128), BF16),
            pltpu.VMEM((COLS, C), BF16),
            pltpu.VMEM((2, 2, NX, 256, 128), F32),
            pltpu.VMEM((2, NX, 256, 128), F32),
            pltpu.VMEM((2, NX - 1, 256, 128), I16),
            pltpu.VMEM((2, NX - 1, 256, 128), I16),
            pltpu.VMEM((2, 256, 128), F32),
            pltpu.VMEM((2, 256, 128), I16),
            pltpu.VMEM((2, NZ - 1, 16, 128), I16),
            pltpu.VMEM((SUB, SHARE, COLS), F32),
            pltpu.VMEM((SUB - 1, SHARE, COLS), F32),
            pltpu.VMEM((8, 16, 128), F32),
            pltpu.VMEM((8, 16, 128), F32),
            pltpu.SemaphoreType.DMA((105,)),
            pltpu.SemaphoreType.DMA((105,)),
            pltpu.SemaphoreType.DMA((6,)),
        ],
        compiler_params=pltpu.CompilerParams(
            collective_id=0, has_side_effects=True, vmem_limit_bytes=56 * 1024 * 1024
        ),
    )(feats, weight, grad_out, neighbors, send_rows, send_counts.T)
    return pl.pallas_call(
        finish,
        out_shape=(
            jax.ShapeDtypeStruct((SHARE, VOX), BF16),
            jax.ShapeDtypeStruct((SHARE, VOX), F32),
            jax.ShapeDtypeStruct((KVOL, SHARE, C), F32),
        ),
        in_specs=[vmem] * 3,
        out_specs=[vmem] * 3,
        compiler_params=pltpu.CompilerParams(vmem_limit_bytes=56 * 1024 * 1024),
    )(*[pltpu.with_memory_space_constraint(one, pltpu.VMEM) for one in (codes, out_feats, grad_feats)])


def solution(mesh):
    in_specs = (
        P("sub", "dom"),
        P(None, "sub", None),
        P("sub", "dom"),
        P(None, "dom"),
        P("dom", None),
        P(),
    )
    out_specs = (P("sub", "dom"), P("sub", "dom"), P(None, "sub", None))
    return jax.shard_map(body, mesh=mesh, in_specs=in_specs, out_specs=out_specs, check_vma=False)
```

```python
import math

import jax
import jax.numpy as jnp
from jax import lax
from jax.experimental import pallas as pl
from jax.experimental.pallas import tpu as pltpu
from jax.sharding import PartitionSpec as P

C = 256
KVOL = 27
CAP = 32
SUB = 4
NX = 4
NZ = 16
DOM = 2 * NX * NZ
SHARE = C // SUB
VOX = 384
HALO = 8 * CAP
COLS = VOX + HALO
GRID_Y = 8
DIRECTIONS = ((-1, -1), (-1, 0), (-1, 1), (0, -1), (0, 1), (1, -1), (1, 0), (1, 1))
HOPS = tuple(dx * GRID_Y + dy for dx, dy in DIRECTIONS)
CHUNKS = ((0, 15), (15, 27))
UNROLL = 3
STEPS = 128.0
TOP = 32000.0
MESH = pl.DeviceIdType.MESH
F32 = jnp.float32
BF16 = jnp.bfloat16
I16 = jnp.int16


def dot(a, b, dims):
    return lax.dot_general(a, b, (dims, ((), ())), preferred_element_type=F32)


NN = ((1,), (0,))
NT = ((1,), (1,))
TN = ((0,), (0,))


def encode(tiles, n):
    row = lax.broadcasted_iota(jnp.int32, tiles.shape, tiles.ndim - 2)
    tiles = jnp.where(row < n, tiles, 0.0)
    top = jnp.max(jnp.abs(tiles), axis=-2, keepdims=True)
    level = jnp.ceil(jnp.log2(jnp.maximum(top, 1e-33)) * STEPS)
    codes = jnp.round(tiles * (jnp.exp2(level * (-1.0 / STEPS)) * TOP))
    return jnp.where(row == n, level, codes).astype(jnp.int32).astype(I16)


def decode(codes, n):
    values = codes.astype(jnp.int32).astype(F32)
    level = values[..., n : n + 1, :]
    return values * (jnp.exp2(level * (1.0 / STEPS)) * (1.0 / TOP))


def kernel(
    feats_hbm, weight_hbm, grad_out_hbm, neighbors_hbm, send_rows_hbm, send_counts_hbm,
    out_feats, grad_feats, codes,
    feats, weight, grad_out, neighbors, send_rows, send_counts,
    nbr_t, onehot, picked, spread_hi, spread_lo, share_all, halo_out, halo_in, halo_all,
    table, wg, pair_in, x_out, x_in, x_sum, z_out, z_in, tg, tg_in, back_out, back_in,
    out_sum, send, recv, local,
):
    me = lax.axis_index("dom")
    sub = lax.axis_index("sub")
    core = lax.rem(me, 2)
    z = lax.rem(me // 2, NZ)
    x = me // (2 * NZ)

    def wrap(i):
        return lax.rem(i + DOM, DOM)

    def at(xx, zz, cc):
        return (xx * NZ + zz) * 2 + cc

    twin = at(x, z, 1 - core)

    def x_peer(d):
        return lax.rem(x + d, NX)

    def z_peer(d):
        return lax.rem(z + d, NZ)

    def far_first(i):
        return NZ // 2 + ((i + 1) // 2) * (2 * lax.rem(i, 2) - 1)

    def y_peer(d):
        return lax.rem(sub + d, SUB)

    slots = {}

    def copy(name, index, src, dst, device):
        base = slots[name]
        return pltpu.make_async_remote_copy(
            src_ref=src, dst_ref=dst, send_sem=send.at[base + index], recv_sem=recv.at[base + index],
            device_id=device, device_id_type=MESH,
        )

    for base, name in enumerate(("share", "fwd", "tg")):
        slots[name] = 3 * base
    slots["halo"], slots["back"] = 9, 17
    slots["pair"], slots["gpair"] = 25, 27
    slots["x"], slots["gx"] = 35, 41
    slots["z"], slots["gz"] = 47, 79

    barrier = pltpu.get_barrier_semaphore()
    peers = [(me, y_peer(d)) for d in range(1, SUB)]
    peers += [(wrap(me + hop), sub) for hop in HOPS]
    peers += [(twin, sub)]
    peers += [(at(x_peer(d), z, core), sub) for d in range(1, NX)]
    def load(i):
        pairs = (
            (send_counts_hbm, send_counts), (send_rows_hbm, send_rows), (feats_hbm, feats),
            (neighbors_hbm, neighbors), (grad_out_hbm, grad_out), (weight_hbm, weight),
        )
        return pltpu.make_async_copy(pairs[i][0], pairs[i][1], local.at[i])

    with jax.named_scope("loads_first"):
        for i in range(3):
            load(i).start()

    with jax.named_scope("barrier_signals"):
        @pl.loop(0, NZ - 1)
        def _(i):
            peer = (at(x, z_peer(far_first(i)), core), sub)
            pl.semaphore_signal(barrier, inc=1, device_id=peer, device_id_type=MESH)

        for peer in peers:
            pl.semaphore_signal(barrier, inc=1, device_id=peer, device_id_type=MESH)

    with jax.named_scope("loads"):
        for i in range(3, 6):
            load(i).start()

    with jax.named_scope("boundary_tiles"):
        for i in range(3):
            load(i).wait()
        lane = lax.broadcasted_iota(jnp.int32, (1, HALO), 1)
        mine = send_counts[...]
        mine = jnp.where(lax.broadcasted_iota(jnp.int32, (8, DOM), 1) == me, mine, 0).astype(F32)
        mine = jnp.sum(mine, axis=1, keepdims=True).astype(jnp.int32)
        count = jnp.zeros((1, HALO), jnp.int32)
        for n in range(8):
            count = jnp.where(lane // CAP == n, mine[n : n + 1, :], count)
        rows = jnp.where(lane % CAP < count, send_rows[...], -1)
        pick = (lax.broadcasted_iota(jnp.int32, (VOX, HALO), 0) == rows).astype(F32).astype(BF16)
        outgoing = dot(feats[...], pick, NN).T.reshape(8, 2, 16, SHARE)
        halo_out[...] = jnp.concatenate([outgoing[:, 0], outgoing[:, 1]], axis=-1).astype(BF16)

    with jax.named_scope("barrier_wait"):
        pl.semaphore_wait(barrier, len(peers) + NZ - 1)

    def share_copy(d):
        return copy("share", d - 1, feats, share_all.at[sub], (me, y_peer(d)))

    def halo_copy(n):
        return copy("halo", n, halo_out.at[n], halo_in.at[n], (wrap(me + HOPS[n]), sub))

    def fwd_copy(d):
        return copy("fwd", d - 1, halo_in, halo_all.at[sub], (me, y_peer(d)))

    with jax.named_scope("first_sends"):
        for n in range(8):
            halo_copy(n).start()
        for d in range(1, SUB):
            share_copy(d).start()
        share_all[sub] = feats[...]

    with jax.named_scope("transpose_maps"):
        for i in (3, 4, 5):
            load(i).wait()
        nbr_t[...] = jnp.concatenate(
            [neighbors[...], jnp.zeros((128 - KVOL, VOX), jnp.int32)], axis=0
        ).T
        col = lax.broadcasted_iota(jnp.int32, (1, COLS), 1)
        r = col - VOX
        slot = jnp.where(col < VOX, col, VOX + ((r % 128) // 16) * CAP + (r // 128) * 16 + r % 16)

    with jax.named_scope("onehot"):
        @pl.loop(0, KVOL // UNROLL)
        def _(g):
            now = nbr_t[...]
            nbr_t[...] = pltpu.roll(now, 128 - UNROLL, 1)
            for j in range(UNROLL):
                onehot[g * UNROLL + j] = (now[:, j : j + 1] == slot).astype(F32).astype(BF16)

    def spread(first, last):
        @pl.loop(first, last)
        def _(g):
            for j in range(UNROLL):
                k = g * UNROLL + j
                total = dot(grad_out[...], onehot[k], NN)
                high = total.astype(BF16)
                spread_hi[k] = high
                spread_lo[k] = (total - high.astype(F32)).astype(BF16)

    with jax.named_scope("spread_a"):
        spread(0, 5)

    def gather_own(first, last):
        @pl.loop(first // UNROLL, last // UNROLL)
        def _(g):
            hot = onehot[pl.ds(g * UNROLL, UNROLL), :, 0:VOX].reshape(UNROLL * VOX, VOX)
            got = dot(hot, table[0:VOX], NN).astype(BF16)
            picked[pl.ds(g * UNROLL, UNROLL)] = got.reshape(UNROLL, VOX, C)

    with jax.named_scope("table_own"):
        for d in range(1, SUB):
            share_copy(d).wait_recv()
        table[0:VOX] = share_all[...].reshape(C, VOX).T
    with jax.named_scope("gather_own_a"):
        gather_own(0, 9)

    with jax.named_scope("wg_rows"):
        for c, (lo, hi) in enumerate(CHUNKS):
            for row in range(hi - lo, 16):
                for cc in range(2):
                    for xx in range(NX):
                        wg[c, cc, xx, pl.ds(row, 16, stride=16), :] = jnp.zeros((16, 128), F32)

    with jax.named_scope("halo_arrival"):
        for n in range(8):
            halo_copy(n).wait_recv()
        for d in range(1, SUB):
            fwd_copy(d).start()
        halo_all[sub] = halo_in[...]

    with jax.named_scope("gather_own_b"):
        gather_own(9, 27)

    with jax.named_scope("table_halo"):
        for d in range(1, SUB):
            fwd_copy(d).wait_recv()
        tiles = halo_all[...].reshape(SUB, 128, 128)
        for half in range(2):
            lanes = slice(half * SHARE, (half + 1) * SHARE)
            table[VOX + half * 128 : VOX + (half + 1) * 128] = jnp.concatenate(
                [tiles[s][:, lanes] for s in range(SUB)], axis=1
            )

    def pair_copy(c):
        return copy("pair", c, wg.at[c, 1 - core], pair_in.at[c], (twin, sub))

    def x_copy(c, d):
        return copy("x", 3 * c + d - 1, x_out.at[c, d - 1], x_in.at[c, d - 1], (at(x_peer(d), z, core), sub))

    def own_tile(zz):
        return pl.ds(pl.multiple_of(zz * 16, 16), 16)

    def z_copy(c, d):
        return copy("z", 16 * c + d - 1, z_out.at[c, own_tile(z_peer(d))], z_in.at[c, d - 1], (at(x, z_peer(d), core), sub))

    def gz_copy(c, d):
        ref = codes.at[c, core, x, own_tile(z)]
        return copy("gz", 16 * c + d - 1, ref, ref, (at(x, z_peer(d), core), sub))

    def gz_arrival(c, d):
        ref = codes.at[c, core, x, own_tile(z_peer(NZ - d))]
        return copy("gz", 16 * c + d - 1, ref, ref, (at(x, z_peer(d), core), sub))

    def gx_copy(c, d):
        ref = codes.at[c, core, x]
        return copy("gx", 3 * c + d - 1, ref, ref, (at(x_peer(d), z, core), sub))

    def gx_arrival(c, d):
        ref = codes.at[c, core, x_peer(NX - d)]
        return copy("gx", 3 * c + d - 1, ref, ref, (at(x_peer(d), z, core), sub))

    def gpair_copy(c, d):
        ref = codes.at[c, core, x_peer(NX - d)]
        return copy("gpair", NX * c + d, ref, ref, (twin, sub))

    def gpair_arrival(c, d):
        ref = codes.at[c, 1 - core, x_peer(NX - d)]
        return copy("gpair", NX * c + d, ref, ref, (twin, sub))

    def gather(c, first, last):
        lo = CHUNKS[c][0]

        @pl.loop(first // UNROLL, last // UNROLL)
        def _(g):
            k0 = g * UNROLL
            hot = onehot[pl.ds(k0, UNROLL), :, VOX:COLS].reshape(UNROLL * VOX, HALO)
            got = dot(hot, table[VOX:COLS], NN).astype(BF16).reshape(UNROLL, VOX, C)
            got = got + picked[pl.ds(k0, UNROLL)]
            picked[pl.ds(k0, UNROLL)] = got
            for j in range(UNROLL):
                fresh = dot(grad_out[...], got[j], NN)
                for cc in range(2):
                    for xx in range(NX):
                        r0, l0 = cc * 32 + (xx // 2) * 16, (xx % 2) * 128
                        wg[c, cc, xx, pl.ds(k0 + j - lo, 16, stride=16), :] = fresh[r0 : r0 + 16, l0 : l0 + 128]

    def pair_to_x(c):
        lo, hi = CHUNKS[c]
        pair_copy(c).wait_recv()
        for d in (2, 1, 3):
            both = wg[c, core, x_peer(d)] + pair_in[c, x_peer(d)]
            x_out[c, d - 1] = encode(both.reshape(16, 16, 128), hi - lo).reshape(256, 128)
            x_copy(c, d).start()

    def x_to_z(c):
        lo, hi = CHUNKS[c]
        for d in range(1, NX):
            x_copy(c, d).wait_recv()
        total = (wg[c, core, x] + pair_in[c, x]).reshape(16, 16, 128)
        for d in range(1, NX):
            total = total + decode(x_in[c, d - 1].reshape(16, 16, 128), hi - lo)
        x_sum[c] = total.reshape(256, 128)
        z_out[c] = encode(total, hi - lo).reshape(256, 128)

        @pl.loop(0, NZ - 1)
        def _(i):
            z_copy(c, far_first(i)).start()

    with jax.named_scope("gather_a"):
        gather(0, 0, 15)
    with jax.named_scope("pair_a"):
        pair_copy(0).start()
    with jax.named_scope("gather_b"):
        gather(1, 15, 21)
    with jax.named_scope("pair_to_x_a"):
        pair_to_x(0)
    with jax.named_scope("gather_c"):
        gather(1, 21, 27)
    with jax.named_scope("pair_b"):
        pair_copy(1).start()

    with jax.named_scope("pair_to_x_b"):
        pair_to_x(1)
    with jax.named_scope("spread_b"):
        spread(5, 9)

    with jax.named_scope("x_to_z_a"):
        x_to_z(0)

    with jax.named_scope("table_grad"):
        total = None
        for k in range(0, KVOL, 4):
            n = min(4, KVOL - k)
            w = weight[k : k + n].reshape(n * SHARE, C)
            for part in (spread_hi, spread_lo):
                term = dot(w, part[k : k + n].reshape(n * SHARE, COLS), TN)
                total = term if total is None else total + term
        tg[...] = total.reshape(SUB, SHARE, COLS)

    def tg_copy(d):
        return copy("tg", d - 1, tg.at[y_peer(d)], tg_in.at[d - 1], (me, y_peer(d)))

    with jax.named_scope("tg_sends"):
        for d in range(1, SUB):
            tg_copy(d).start()

    with jax.named_scope("x_to_z_b"):
        x_to_z(1)

    def z_reduce(c):
        lo, hi = CHUNKS[c]

        @pl.loop(1, NZ)
        def _(d):
            z_copy(c, d).wait_recv()

        total = x_sum[c, own_tile(z)] + jnp.sum(decode(z_in[c], hi - lo), axis=0)
        scaled = total * (1.0 / math.sqrt(VOX * DOM))
        codes[c, core, x, own_tile(z)] = encode(scaled, hi - lo)

        @pl.loop(0, NZ - 1)
        def _(i):
            gz_copy(c, far_first(i)).start()

    def z_to_x(c):
        @pl.loop(1, NZ)
        def _(d):
            gz_arrival(c, d).wait_recv()

        for d in (2, 1, 3):
            gx_copy(c, d).start()
        gpair_copy(c, 0).start()

    def x_to_pair(c):
        for d in (1, 3, 2):
            gx_arrival(c, d).wait_recv()
            gpair_copy(c, d).start()

    def out_step(g, acc):
        for j in range(UNROLL):
            acc = acc + dot(weight[g * UNROLL + j], picked[g * UNROLL + j], NT)
        return acc

    with jax.named_scope("out_feats_a"):
        out_sum[...] = lax.fori_loop(0, 5, out_step, jnp.zeros((SHARE, VOX), F32))
    with jax.named_scope("z_reduce_a"):
        z_reduce(0)

    with jax.named_scope("tg_sum"):
        for d in range(1, SUB):
            tg_copy(d).wait_recv()
        mine_tg = tg[sub] + tg_in[0] + tg_in[1] + tg_in[2]
        tail = mine_tg[:, VOX:].T
        back_out[...] = jnp.concatenate([tail[:128], tail[128:]], axis=1).reshape(8, 16, 128)

    def back_copy(n):
        return copy("back", n, back_out.at[n], back_in.at[n], (wrap(me - HOPS[n]), sub))

    with jax.named_scope("back_sends"):
        for n in range(8):
            back_copy(n).start()

    with jax.named_scope("z_reduce_b"):
        z_reduce(1)

    with jax.named_scope("out_feats_b"):
        out_feats[...] = lax.fori_loop(5, 9, out_step, out_sum[...]).astype(BF16)

    with jax.named_scope("z_back"):
        z_to_x(0)
        z_to_x(1)
    with jax.named_scope("drain_early"):
        for d in range(1, SUB):
            share_copy(d).wait_send()
            fwd_copy(d).wait_send()
            tg_copy(d).wait_send()
        for n in range(8):
            halo_copy(n).wait_send()
            back_copy(n).wait_send()
        for c in range(2):
            pair_copy(c).wait_send()
            for d in range(1, NX):
                x_copy(c, d).wait_send()

            @pl.loop(1, NZ)
            def _(d):
                z_copy(c, d).wait_send()
                gz_copy(c, d).wait_send()

    with jax.named_scope("x_back"):
        x_to_pair(0)
        x_to_pair(1)

    with jax.named_scope("grad_feats"):
        for n in range(8):
            back_copy(n).wait_recv()
        back = back_in[...]
        back = jnp.concatenate([back[:, :, :SHARE][:, None], back[:, :, SHARE:][:, None]], axis=1)
        back = back.reshape(HALO, SHARE).T
        back_hi = back.astype(BF16)
        back_lo = (back - back_hi.astype(F32)).astype(BF16)
        grad_feats[...] = mine_tg[:, :VOX] + dot(back_hi, pick, NT) + dot(back_lo, pick, NT)

    with jax.named_scope("pair_back"):
        for c in range(2):
            for d in range(NX):
                gpair_arrival(c, d).wait_recv()

    with jax.named_scope("drain"):
        for c in range(2):
            for d in range(NX):
                gpair_copy(c, d).wait_send()
            for d in range(1, NX):
                gx_copy(c, d).wait_send()


def finish(codes, out_in, feats_in, out_feats, grad_feats, grad_weight):
    out_feats[...] = out_in[...]
    grad_feats[...] = feats_in[...]
    for c, (lo, hi) in enumerate(CHUNKS):
        for cc in range(2):
            for xx in range(NX):
                values = decode(codes[c, cc, xx].reshape(16, 16, 128), hi - lo)
                r0, l0 = cc * 32 + (xx // 2) * 16, (xx % 2) * 128
                values = jnp.swapaxes(values, 0, 1)
                grad_weight[lo:hi, r0 : r0 + 16, l0 : l0 + 128] = values[: hi - lo]


def body(feats, weight, grad_out, neighbors, send_rows, send_counts):
    hbm = pl.BlockSpec(memory_space=pltpu.HBM)
    vmem = pl.BlockSpec(memory_space=pltpu.VMEM)
    out_feats, grad_feats, codes = pl.pallas_call(
        kernel,
        out_shape=(
            pltpu.VMEM((SHARE, VOX), BF16),
            pltpu.VMEM((SHARE, VOX), F32),
            pltpu.VMEM((2, 2, NX, 256, 128), I16),
        ),
        in_specs=[hbm] * 6,
        out_specs=[vmem] * 3,
        scratch_shapes=[
            pltpu.VMEM((SHARE, VOX), BF16),
            pltpu.VMEM((KVOL, SHARE, C), BF16),
            pltpu.VMEM((SHARE, VOX), BF16),
            pltpu.VMEM((KVOL, VOX), jnp.int32),
            pltpu.VMEM((1, HALO), jnp.int32),
            pltpu.VMEM((8, DOM), jnp.int32),
            pltpu.VMEM((VOX, 128), jnp.int32),
            pltpu.VMEM((KVOL, VOX, COLS), BF16),
            pltpu.VMEM((KVOL, VOX, C), BF16),
            pltpu.VMEM((KVOL + 1, SHARE, COLS), BF16),
            pltpu.VMEM((KVOL + 1, SHARE, COLS), BF16),
            pltpu.VMEM((SUB, SHARE, VOX), BF16),
            pltpu.VMEM((8, 16, 128), BF16),
            pltpu.VMEM((8, 16, 128), BF16),
            pltpu.VMEM((SUB, 8, 16, 128), BF16),
            pltpu.VMEM((COLS, C), BF16),
            pltpu.VMEM((2, 2, NX, 256, 128), F32),
            pltpu.VMEM((2, NX, 256, 128), F32),
            pltpu.VMEM((2, NX - 1, 256, 128), I16),
            pltpu.VMEM((2, NX - 1, 256, 128), I16),
            pltpu.VMEM((2, 256, 128), F32),
            pltpu.VMEM((2, 256, 128), I16),
            pltpu.VMEM((2, NZ - 1, 16, 128), I16),
            pltpu.VMEM((SUB, SHARE, COLS), F32),
            pltpu.VMEM((SUB - 1, SHARE, COLS), F32),
            pltpu.VMEM((8, 16, 128), F32),
            pltpu.VMEM((8, 16, 128), F32),
            pltpu.VMEM((SHARE, VOX), F32),
            pltpu.SemaphoreType.DMA((111,)),
            pltpu.SemaphoreType.DMA((111,)),
            pltpu.SemaphoreType.DMA((6,)),
        ],
        compiler_params=pltpu.CompilerParams(
            collective_id=0, has_side_effects=True, vmem_limit_bytes=56 * 1024 * 1024
        ),
    )(feats, weight, grad_out, neighbors, send_rows, send_counts.T)
    return pl.pallas_call(
        finish,
        out_shape=(
            jax.ShapeDtypeStruct((SHARE, VOX), BF16),
            jax.ShapeDtypeStruct((SHARE, VOX), F32),
            jax.ShapeDtypeStruct((KVOL, SHARE, C), F32),
        ),
        in_specs=[vmem] * 3,
        out_specs=[vmem] * 3,
        compiler_params=pltpu.CompilerParams(vmem_limit_bytes=56 * 1024 * 1024),
    )(*[pltpu.with_memory_space_constraint(one, pltpu.VMEM) for one in (codes, out_feats, grad_feats)])


def solution(mesh):
    in_specs = (
        P("sub", "dom"),
        P(None, "sub", None),
        P("sub", "dom"),
        P(None, "dom"),
        P("dom", None),
        P(),
    )
    out_specs = (P("sub", "dom"), P("sub", "dom"), P(None, "sub", None))
    return jax.shard_map(body, mesh=mesh, in_specs=in_specs, out_specs=out_specs, check_vma=False)
```

```python
import math

import jax
import jax.numpy as jnp
from jax import lax
from jax.experimental import pallas as pl
from jax.experimental.pallas import tpu as pltpu
from jax.sharding import PartitionSpec as P

C = 256
KVOL = 27
CAP = 32
SUB = 4
NX = 4
NZ = 16
DOM = 2 * NX * NZ
SHARE = C // SUB
VOX = 384
HALO = 8 * CAP
COLS = VOX + HALO
GRID_Y = 8
DIRECTIONS = ((-1, -1), (-1, 0), (-1, 1), (0, -1), (0, 1), (1, -1), (1, 0), (1, 1))
HOPS = tuple(dx * GRID_Y + dy for dx, dy in DIRECTIONS)
CHUNKS = ((0, 15), (15, 27))
UNROLL = 3
STEPS = 128.0
TOP = 32000.0
MESH = pl.DeviceIdType.MESH
F32 = jnp.float32
BF16 = jnp.bfloat16
I16 = jnp.int16


def dot(a, b, dims):
    return lax.dot_general(a, b, (dims, ((), ())), preferred_element_type=F32)


NN = ((1,), (0,))
NT = ((1,), (1,))
TN = ((0,), (0,))


def encode(tiles, n):
    row = lax.broadcasted_iota(jnp.int32, tiles.shape, tiles.ndim - 2)
    tiles = jnp.where(row < n, tiles, 0.0)
    top = jnp.max(jnp.abs(tiles), axis=-2, keepdims=True)
    level = jnp.ceil(jnp.log2(jnp.maximum(top, 1e-33)) * STEPS)
    codes = jnp.round(tiles * (jnp.exp2(level * (-1.0 / STEPS)) * TOP))
    return jnp.where(row == n, level, codes).astype(jnp.int32).astype(I16)


def decode(codes, n):
    values = codes.astype(jnp.int32).astype(F32)
    level = values[..., n : n + 1, :]
    return values * (jnp.exp2(level * (1.0 / STEPS)) * (1.0 / TOP))


def kernel(
    feats_hbm, weight_hbm, grad_out_hbm, neighbors_hbm, send_rows_hbm, send_counts_hbm,
    out_feats, grad_feats, codes,
    feats, weight, grad_out, neighbors, send_rows, send_counts,
    nbr_t, onehot, picked, spread_hi, spread_lo, share_all, halo_out, halo_in, halo_all,
    table, wg, pair_in, x_out, x_in, x_sum, z_out, z_in, tg, tg_in, back_out, back_in,
    out_sum, send, recv, local,
):
    me = lax.axis_index("dom")
    sub = lax.axis_index("sub")
    core = lax.rem(me, 2)
    z = lax.rem(me // 2, NZ)
    x = me // (2 * NZ)

    def wrap(i):
        return lax.rem(i + DOM, DOM)

    def at(xx, zz, cc):
        return (xx * NZ + zz) * 2 + cc

    twin = at(x, z, 1 - core)

    def x_peer(d):
        return lax.rem(x + d, NX)

    def z_peer(d):
        return lax.rem(z + d, NZ)

    def far_first(i):
        return NZ // 2 + ((i + 1) // 2) * (2 * lax.rem(i, 2) - 1)

    def y_peer(d):
        return lax.rem(sub + d, SUB)

    slots = {}

    def copy(name, index, src, dst, device):
        base = slots[name]
        return pltpu.make_async_remote_copy(
            src_ref=src, dst_ref=dst, send_sem=send.at[base + index], recv_sem=recv.at[base + index],
            device_id=device, device_id_type=MESH,
        )

    for base, name in enumerate(("share", "fwd", "tg")):
        slots[name] = 3 * base
    slots["halo"], slots["back"] = 9, 17
    slots["pair"], slots["gpair"] = 25, 27
    slots["x"], slots["gx"] = 35, 41
    slots["z"], slots["gz"] = 47, 79

    barrier = pltpu.get_barrier_semaphore()
    peers = [(me, y_peer(d)) for d in range(1, SUB)]
    peers += [(wrap(me + hop), sub) for hop in HOPS]
    peers += [(twin, sub)]
    peers += [(at(x_peer(d), z, core), sub) for d in range(1, NX)]
    def load(i):
        pairs = (
            (send_counts_hbm, send_counts), (send_rows_hbm, send_rows), (feats_hbm, feats),
            (neighbors_hbm, neighbors), (grad_out_hbm, grad_out), (weight_hbm, weight),
        )
        return pltpu.make_async_copy(pairs[i][0], pairs[i][1], local.at[i])

    with jax.named_scope("loads_first"):
        for i in range(3):
            load(i).start()

    with jax.named_scope("barrier_signals"):
        @pl.loop(0, NZ - 1)
        def _(i):
            peer = (at(x, z_peer(far_first(i)), core), sub)
            pl.semaphore_signal(barrier, inc=1, device_id=peer, device_id_type=MESH)

        for peer in peers:
            pl.semaphore_signal(barrier, inc=1, device_id=peer, device_id_type=MESH)

    with jax.named_scope("loads"):
        for i in range(3, 6):
            load(i).start()

    with jax.named_scope("boundary_tiles"):
        for i in range(3):
            load(i).wait()
        lane = lax.broadcasted_iota(jnp.int32, (1, HALO), 1)
        mine = send_counts[...]
        mine = jnp.where(lax.broadcasted_iota(jnp.int32, (8, DOM), 1) == me, mine, 0).astype(F32)
        mine = jnp.sum(mine, axis=1, keepdims=True).astype(jnp.int32)
        count = jnp.zeros((1, HALO), jnp.int32)
        for n in range(8):
            count = jnp.where(lane // CAP == n, mine[n : n + 1, :], count)
        rows = jnp.where(lane % CAP < count, send_rows[...], -1)
        pick = (lax.broadcasted_iota(jnp.int32, (VOX, HALO), 0) == rows).astype(F32).astype(BF16)
        outgoing = dot(feats[...], pick, NN).T.reshape(8, 2, 16, SHARE)
        halo_out[...] = jnp.concatenate([outgoing[:, 0], outgoing[:, 1]], axis=-1).astype(BF16)

    with jax.named_scope("barrier_wait"):
        pl.semaphore_wait(barrier, len(peers) + NZ - 1)

    def share_copy(d):
        return copy("share", d - 1, feats, share_all.at[sub], (me, y_peer(d)))

    def halo_copy(n):
        return copy("halo", n, halo_out.at[n], halo_in.at[n], (wrap(me + HOPS[n]), sub))

    def fwd_copy(d):
        return copy("fwd", d - 1, halo_in, halo_all.at[sub], (me, y_peer(d)))

    with jax.named_scope("first_sends"):
        for n in range(8):
            halo_copy(n).start()
        for d in range(1, SUB):
            share_copy(d).start()
        share_all[sub] = feats[...]

    with jax.named_scope("transpose_maps"):
        for i in (3, 4, 5):
            load(i).wait()
        nbr_t[...] = jnp.concatenate(
            [neighbors[...], jnp.zeros((128 - KVOL, VOX), jnp.int32)], axis=0
        ).T
        col = lax.broadcasted_iota(jnp.int32, (1, COLS), 1)
        r = col - VOX
        slot = jnp.where(col < VOX, col, VOX + ((r % 128) // 16) * CAP + (r // 128) * 16 + r % 16)

    with jax.named_scope("onehot"):
        @pl.loop(0, KVOL // UNROLL)
        def _(g):
            now = nbr_t[...]
            nbr_t[...] = pltpu.roll(now, 128 - UNROLL, 1)
            for j in range(UNROLL):
                onehot[g * UNROLL + j] = (now[:, j : j + 1] == slot).astype(F32).astype(BF16)

    def spread(first, last):
        @pl.loop(first, last)
        def _(g):
            for j in range(UNROLL):
                k = g * UNROLL + j
                total = dot(grad_out[...], onehot[k], NN)
                high = total.astype(BF16)
                spread_hi[k] = high
                spread_lo[k] = (total - high.astype(F32)).astype(BF16)

    with jax.named_scope("spread_a"):
        spread(0, 5)

    def gather_own(first, last):
        @pl.loop(first // UNROLL, last // UNROLL)
        def _(g):
            hot = onehot[pl.ds(g * UNROLL, UNROLL), :, 0:VOX].reshape(UNROLL * VOX, VOX)
            got = dot(hot, table[0:VOX], NN).astype(BF16)
            picked[pl.ds(g * UNROLL, UNROLL)] = got.reshape(UNROLL, VOX, C)

    with jax.named_scope("table_own"):
        for d in range(1, SUB):
            share_copy(d).wait_recv()
        table[0:VOX] = share_all[...].reshape(C, VOX).T
    with jax.named_scope("gather_own_a"):
        gather_own(0, 9)

    with jax.named_scope("wg_rows"):
        for c, (lo, hi) in enumerate(CHUNKS):
            for row in range(hi - lo, 16):
                for cc in range(2):
                    for xx in range(NX):
                        wg[c, cc, xx, pl.ds(row, 16, stride=16), :] = jnp.zeros((16, 128), F32)

    with jax.named_scope("halo_arrival"):
        for n in range(8):
            halo_copy(n).wait_recv()
        for d in range(1, SUB):
            fwd_copy(d).start()
        halo_all[sub] = halo_in[...]

    with jax.named_scope("gather_own_b"):
        gather_own(9, 27)

    with jax.named_scope("table_halo"):
        for d in range(1, SUB):
            fwd_copy(d).wait_recv()
        tiles = halo_all[...].reshape(SUB, 128, 128)
        for half in range(2):
            lanes = slice(half * SHARE, (half + 1) * SHARE)
            table[VOX + half * 128 : VOX + (half + 1) * 128] = jnp.concatenate(
                [tiles[s][:, lanes] for s in range(SUB)], axis=1
            )

    def pair_copy(c):
        return copy("pair", c, wg.at[c, 1 - core], pair_in.at[c], (twin, sub))

    def x_copy(c, d):
        return copy("x", 3 * c + d - 1, x_out.at[c, d - 1], x_in.at[c, d - 1], (at(x_peer(d), z, core), sub))

    def own_tile(zz):
        return pl.ds(pl.multiple_of(zz * 16, 16), 16)

    def z_copy(c, d):
        return copy("z", 16 * c + d - 1, z_out.at[c, own_tile(z_peer(d))], z_in.at[c, d - 1], (at(x, z_peer(d), core), sub))

    def gz_copy(c, d):
        ref = codes.at[c, core, x, own_tile(z)]
        return copy("gz", 16 * c + d - 1, ref, ref, (at(x, z_peer(d), core), sub))

    def gz_arrival(c, d):
        ref = codes.at[c, core, x, own_tile(z_peer(NZ - d))]
        return copy("gz", 16 * c + d - 1, ref, ref, (at(x, z_peer(d), core), sub))

    def gx_copy(c, d):
        ref = codes.at[c, core, x]
        return copy("gx", 3 * c + d - 1, ref, ref, (at(x_peer(d), z, core), sub))

    def gx_arrival(c, d):
        ref = codes.at[c, core, x_peer(NX - d)]
        return copy("gx", 3 * c + d - 1, ref, ref, (at(x_peer(d), z, core), sub))

    def gpair_copy(c, d):
        ref = codes.at[c, core, x_peer(NX - d)]
        return copy("gpair", NX * c + d, ref, ref, (twin, sub))

    def gpair_arrival(c, d):
        ref = codes.at[c, 1 - core, x_peer(NX - d)]
        return copy("gpair", NX * c + d, ref, ref, (twin, sub))

    def gather(c, first, last):
        lo = CHUNKS[c][0]

        @pl.loop(first // UNROLL, last // UNROLL)
        def _(g):
            k0 = g * UNROLL
            hot = onehot[pl.ds(k0, UNROLL), :, VOX:COLS].reshape(UNROLL * VOX, HALO)
            got = dot(hot, table[VOX:COLS], NN).astype(BF16).reshape(UNROLL, VOX, C)
            got = got + picked[pl.ds(k0, UNROLL)]
            picked[pl.ds(k0, UNROLL)] = got
            for j in range(UNROLL):
                fresh = dot(grad_out[...], got[j], NN)
                for cc in range(2):
                    for xx in range(NX):
                        r0, l0 = cc * 32 + (xx // 2) * 16, (xx % 2) * 128
                        wg[c, cc, xx, pl.ds(k0 + j - lo, 16, stride=16), :] = fresh[r0 : r0 + 16, l0 : l0 + 128]

    def pair_to_x(c):
        lo, hi = CHUNKS[c]
        pair_copy(c).wait_recv()
        for d in (2, 1, 3):
            both = wg[c, core, x_peer(d)] + pair_in[c, x_peer(d)]
            x_out[c, d - 1] = encode(both.reshape(16, 16, 128), hi - lo).reshape(256, 128)
            x_copy(c, d).start()

    def x_to_z(c):
        lo, hi = CHUNKS[c]
        total = (wg[c, core, x] + pair_in[c, x]).reshape(16, 16, 128)
        for d in (1, 3, 2):
            x_copy(c, d).wait_recv()
            total = total + decode(x_in[c, d - 1].reshape(16, 16, 128), hi - lo)
        x_sum[c] = total.reshape(256, 128)
        z_out[c] = encode(total, hi - lo).reshape(256, 128)

        @pl.loop(0, NZ - 1)
        def _(i):
            z_copy(c, far_first(i)).start()

    with jax.named_scope("gather_a"):
        gather(0, 0, 15)
    with jax.named_scope("pair_a"):
        pair_copy(0).start()
    with jax.named_scope("gather_b"):
        gather(1, 15, 21)
    with jax.named_scope("pair_to_x_a"):
        pair_to_x(0)
    with jax.named_scope("gather_c"):
        gather(1, 21, 27)
    with jax.named_scope("pair_b"):
        pair_copy(1).start()

    with jax.named_scope("pair_to_x_b"):
        pair_to_x(1)
    with jax.named_scope("spread_b"):
        spread(5, 9)

    with jax.named_scope("x_to_z_a"):
        x_to_z(0)

    with jax.named_scope("table_grad"):
        total = None
        for k in range(0, KVOL, 4):
            n = min(4, KVOL - k)
            w = weight[k : k + n].reshape(n * SHARE, C)
            for part in (spread_hi, spread_lo):
                term = dot(w, part[k : k + n].reshape(n * SHARE, COLS), TN)
                total = term if total is None else total + term
        tg[...] = total.reshape(SUB, SHARE, COLS)

    def tg_copy(d):
        return copy("tg", d - 1, tg.at[y_peer(d)], tg_in.at[d - 1], (me, y_peer(d)))

    with jax.named_scope("tg_sends"):
        for d in range(1, SUB):
            tg_copy(d).start()

    with jax.named_scope("x_to_z_b"):
        x_to_z(1)

    def z_reduce(c):
        lo, hi = CHUNKS[c]

        total = x_sum[c, own_tile(z)]
        for first, last in ((1, 5), (12, 16), (5, 12)):
            @pl.loop(first, last)
            def _(d):
                z_copy(c, d).wait_recv()

            total = total + jnp.sum(decode(z_in[c, first - 1 : last - 1], hi - lo), axis=0)
        scaled = total * (1.0 / math.sqrt(VOX * DOM))
        codes[c, core, x, own_tile(z)] = encode(scaled, hi - lo)

        @pl.loop(0, NZ - 1)
        def _(i):
            gz_copy(c, far_first(i)).start()

    def z_to_x(c):
        @pl.loop(1, NZ)
        def _(d):
            gz_arrival(c, d).wait_recv()

        for d in (2, 1, 3):
            gx_copy(c, d).start()
        gpair_copy(c, 0).start()

    def x_to_pair(c):
        for d in (1, 3, 2):
            gx_arrival(c, d).wait_recv()
            gpair_copy(c, d).start()

    def out_step(g, acc):
        for j in range(UNROLL):
            acc = acc + dot(weight[g * UNROLL + j], picked[g * UNROLL + j], NT)
        return acc

    with jax.named_scope("out_feats_a"):
        out_sum[...] = lax.fori_loop(0, 5, out_step, jnp.zeros((SHARE, VOX), F32))
    with jax.named_scope("z_reduce_a"):
        z_reduce(0)

    with jax.named_scope("tg_sum"):
        for d in range(1, SUB):
            tg_copy(d).wait_recv()
        mine_tg = tg[sub] + tg_in[0] + tg_in[1] + tg_in[2]
        tail = mine_tg[:, VOX:].T
        back_out[...] = jnp.concatenate([tail[:128], tail[128:]], axis=1).reshape(8, 16, 128)

    def back_copy(n):
        return copy("back", n, back_out.at[n], back_in.at[n], (wrap(me - HOPS[n]), sub))

    with jax.named_scope("back_sends"):
        for n in range(8):
            back_copy(n).start()

    with jax.named_scope("z_reduce_b"):
        z_reduce(1)

    with jax.named_scope("out_feats_b"):
        out_feats[...] = lax.fori_loop(5, 9, out_step, out_sum[...]).astype(BF16)

    with jax.named_scope("z_back"):
        z_to_x(0)
        z_to_x(1)
    with jax.named_scope("drain_early"):
        for d in range(1, SUB):
            share_copy(d).wait_send()
            fwd_copy(d).wait_send()
            tg_copy(d).wait_send()
        for n in range(8):
            halo_copy(n).wait_send()
            back_copy(n).wait_send()
        for c in range(2):
            pair_copy(c).wait_send()
            for d in range(1, NX):
                x_copy(c, d).wait_send()

            @pl.loop(1, NZ)
            def _(d):
                z_copy(c, d).wait_send()
                gz_copy(c, d).wait_send()

    with jax.named_scope("x_back"):
        x_to_pair(0)
        x_to_pair(1)

    with jax.named_scope("grad_feats"):
        for n in range(8):
            back_copy(n).wait_recv()
        back = back_in[...]
        back = jnp.concatenate([back[:, :, :SHARE][:, None], back[:, :, SHARE:][:, None]], axis=1)
        back = back.reshape(HALO, SHARE).T
        back_hi = back.astype(BF16)
        back_lo = (back - back_hi.astype(F32)).astype(BF16)
        grad_feats[...] = mine_tg[:, :VOX] + dot(back_hi, pick, NT) + dot(back_lo, pick, NT)

    with jax.named_scope("pair_back"):
        for c in range(2):
            for d in range(NX):
                gpair_arrival(c, d).wait_recv()

    with jax.named_scope("drain"):
        for c in range(2):
            for d in range(NX):
                gpair_copy(c, d).wait_send()
            for d in range(1, NX):
                gx_copy(c, d).wait_send()


def finish(codes, out_in, feats_in, out_feats, grad_feats, grad_weight):
    out_feats[...] = out_in[...]
    grad_feats[...] = feats_in[...]
    for c, (lo, hi) in enumerate(CHUNKS):
        for cc in range(2):
            for xx in range(NX):
                values = decode(codes[c, cc, xx].reshape(16, 16, 128), hi - lo)
                r0, l0 = cc * 32 + (xx // 2) * 16, (xx % 2) * 128
                values = jnp.swapaxes(values, 0, 1)
                grad_weight[lo:hi, r0 : r0 + 16, l0 : l0 + 128] = values[: hi - lo]


def body(feats, weight, grad_out, neighbors, send_rows, send_counts):
    hbm = pl.BlockSpec(memory_space=pltpu.HBM)
    vmem = pl.BlockSpec(memory_space=pltpu.VMEM)
    out_feats, grad_feats, codes = pl.pallas_call(
        kernel,
        out_shape=(
            pltpu.VMEM((SHARE, VOX), BF16),
            pltpu.VMEM((SHARE, VOX), F32),
            pltpu.VMEM((2, 2, NX, 256, 128), I16),
        ),
        in_specs=[hbm] * 6,
        out_specs=[vmem] * 3,
        scratch_shapes=[
            pltpu.VMEM((SHARE, VOX), BF16),
            pltpu.VMEM((KVOL, SHARE, C), BF16),
            pltpu.VMEM((SHARE, VOX), BF16),
            pltpu.VMEM((KVOL, VOX), jnp.int32),
            pltpu.VMEM((1, HALO), jnp.int32),
            pltpu.VMEM((8, DOM), jnp.int32),
            pltpu.VMEM((VOX, 128), jnp.int32),
            pltpu.VMEM((KVOL, VOX, COLS), BF16),
            pltpu.VMEM((KVOL, VOX, C), BF16),
            pltpu.VMEM((KVOL + 1, SHARE, COLS), BF16),
            pltpu.VMEM((KVOL + 1, SHARE, COLS), BF16),
            pltpu.VMEM((SUB, SHARE, VOX), BF16),
            pltpu.VMEM((8, 16, 128), BF16),
            pltpu.VMEM((8, 16, 128), BF16),
            pltpu.VMEM((SUB, 8, 16, 128), BF16),
            pltpu.VMEM((COLS, C), BF16),
            pltpu.VMEM((2, 2, NX, 256, 128), F32),
            pltpu.VMEM((2, NX, 256, 128), F32),
            pltpu.VMEM((2, NX - 1, 256, 128), I16),
            pltpu.VMEM((2, NX - 1, 256, 128), I16),
            pltpu.VMEM((2, 256, 128), F32),
            pltpu.VMEM((2, 256, 128), I16),
            pltpu.VMEM((2, NZ - 1, 16, 128), I16),
            pltpu.VMEM((SUB, SHARE, COLS), F32),
            pltpu.VMEM((SUB - 1, SHARE, COLS), F32),
            pltpu.VMEM((8, 16, 128), F32),
            pltpu.VMEM((8, 16, 128), F32),
            pltpu.VMEM((SHARE, VOX), F32),
            pltpu.SemaphoreType.DMA((111,)),
            pltpu.SemaphoreType.DMA((111,)),
            pltpu.SemaphoreType.DMA((6,)),
        ],
        compiler_params=pltpu.CompilerParams(
            collective_id=0, has_side_effects=True, vmem_limit_bytes=56 * 1024 * 1024
        ),
    )(feats, weight, grad_out, neighbors, send_rows, send_counts.T)
    return pl.pallas_call(
        finish,
        out_shape=(
            jax.ShapeDtypeStruct((SHARE, VOX), BF16),
            jax.ShapeDtypeStruct((SHARE, VOX), F32),
            jax.ShapeDtypeStruct((KVOL, SHARE, C), F32),
        ),
        in_specs=[vmem] * 3,
        out_specs=[vmem] * 3,
        compiler_params=pltpu.CompilerParams(vmem_limit_bytes=56 * 1024 * 1024),
    )(*[pltpu.with_memory_space_constraint(one, pltpu.VMEM) for one in (codes, out_feats, grad_feats)])


def solution(mesh):
    in_specs = (
        P("sub", "dom"),
        P(None, "sub", None),
        P("sub", "dom"),
        P(None, "dom"),
        P("dom", None),
        P(),
    )
    out_specs = (P("sub", "dom"), P("sub", "dom"), P(None, "sub", None))
    return jax.shard_map(body, mesh=mesh, in_specs=in_specs, out_specs=out_specs, check_vma=False)
```
